32 devices in a mesh: qrow: 8 (over z, core), kcol: 4 (over y, x).
Axes of the slice: x: 2, y: 2, z: 4, core: 2. Of those that a mesh axis runs over, the one named last changes fastest.
Arguments:
- queries: bfloat16 [4096, 1024], P(('kcol', 'qrow')), may hold values from -105 to 105
- keys: bfloat16 [4096, 256], P(('qrow', 'kcol')), may hold values from -3.5 to 3.5
- values: bfloat16 [4096, 256], P(('qrow', 'kcol')), may hold values from -6 to 6
- outputs: bfloat16 [4096, 1024], P(('kcol', 'qrow')), may hold values from -6 to 6
- out_grad: bfloat16 [4096, 1024], P(('kcol', 'qrow')), may hold values from -6 to 6
- positions: int32 [4096], replicated, may hold values from 0 to 4095, as said below
Outputs:
- query_grad: bfloat16 [4096, 1024], P(('kcol', 'qrow'))
- key_grad: bfloat16 [4096, 256], P(('qrow', 'kcol'))
- value_grad: bfloat16 [4096, 256], P(('qrow', 'kcol'))
The draws below stay inside these ranges and needn't reach their ends.
Inputs may be any that keep to these rules, and one draw needn't show every extreme that they name: positions is a permutation of the 4096 positions; each aligned run of 64 stored rows holds consecutive positions in increasing order, the first a multiple of 64.
All inputs are finite; a program needn't handle non-finite values.
Results may differ from the reference program's by a relative error of at most 0.0048.
Values may be sent and summed in bfloat16 or wider, within the bound.
A program may use at most 128 MiB of HBM per device.

```python
import math
import jax
import jax.numpy as jnp
from jax import lax

HEADS = 16
KV_HEADS = 4
HEAD = 64
STRETCH = 64
TOKENS = 4096


def paired_keys(key, strength):
    base = jnp.clip(jax.random.normal(key, (TOKENS, KV_HEADS * HEAD), jnp.float32), -3.5, 3.5)
    stored = jnp.arange(TOKENS)
    phase = stored % (4 * STRETCH)
    level = 10.0 * (1.0 + (stored // (4 * STRETCH) % 3).astype(jnp.float32))
    leading = (phase == 5) & (strength > 0.5)
    before = (phase == 4) & (strength > 0.5)
    shifted = jnp.roll(base, -1, axis=0)
    shrink = 1.0 - 0.18 / level
    paired = jnp.where(before[:, None], shifted * shrink[:, None], base)
    return (paired, leading, level)


def draw_keys(key, part):
    paired, leading, level = paired_keys(key, 0.0)
    return paired.astype(jnp.bfloat16)


def draw_queries(key, part):
    paired, leading, level = paired_keys(key, 0.0)
    key = jax.random.fold_in(key, 11)
    members = HEADS // KV_HEADS
    own_draw = jnp.clip(jax.random.normal(key, (TOKENS, HEADS * HEAD), jnp.float32), -3.5, 3.5)
    spread = jnp.repeat(paired.reshape(TOKENS, KV_HEADS, 1, HEAD), members, axis=2).reshape(TOKENS, HEADS * HEAD)
    spread = spread * level[:, None]
    return jnp.where(leading[:, None], spread, own_draw).astype(jnp.bfloat16)


def draw_positions(key, part):
    key = jax.random.fold_in(key, 7)
    order = jax.random.permutation(key, TOKENS // STRETCH).astype(jnp.int32)
    stored = jnp.arange(TOKENS, dtype=jnp.int32)
    return (order[stored // STRETCH] * STRETCH + stored % STRETCH).astype(jnp.int32)


def steps_of(own_key, shape, split, low, largest):
    def one(axis_at, blocks):
        heights = jax.random.uniform(jax.random.fold_in(jax.random.fold_in(own_key, 6), axis_at), (blocks,), jnp.float32, low / len(split), largest / len(split))
        return jnp.repeat(jnp.exp(heights), shape[axis_at] // blocks).reshape((-1,) + (1,) * (len(shape) - axis_at - 1))

    level = one(*split[0])
    for cut in split[1:]:
        level = level * one(*cut)
    return level


def bell_draw(stream_key, dims, deviation, most, split=(), kind=jnp.bfloat16):
    gain = steps_of(stream_key, dims, split, -0.22, 0.18) if split else 1.0
    drawn = jax.random.normal(stream_key, dims, jnp.float32) * deviation * gain
    return jnp.minimum(jnp.maximum(drawn, -most), most).astype(kind)


def setup_inputs(seed: int = 0) -> dict:
    streams_of = jax.random.split(jax.random.key(seed), 7)
    return {
        "queries": draw_queries(jax.random.fold_in(streams_of[6], 71), 0),
        "keys": draw_keys(jax.random.fold_in(streams_of[6], 71), 0),
        "values": bell_draw(streams_of[2], (TOKENS, KV_HEADS * HEAD), 1.0, 6.0, ((0, 32),)),
        "outputs": bell_draw(streams_of[3], (TOKENS, HEADS * HEAD), 1.0, 6.0, ((0, 32),)),
        "out_grad": bell_draw(streams_of[4], (TOKENS, HEADS * HEAD), 1.0, 6.0, ((0, 32),)),
        "positions": draw_positions(jax.random.fold_in(streams_of[6], 71), 0),
    }


def reference(queries, keys, values, outputs, out_grad, positions):
    factor = 1.0 / math.sqrt(HEAD)
    members = HEADS // KV_HEADS
    block = math.gcd(TOKENS, 1024)
    blocks = TOKENS // block
    delta = lax.optimization_barrier(jnp.sum(out_grad.astype(jnp.float32).reshape(TOKENS, HEADS, HEAD) * outputs.astype(jnp.float32).reshape(TOKENS, HEADS, HEAD), axis=2))

    def one_group(kv_index):
        key_cols = lax.dynamic_slice_in_dim(keys, kv_index * HEAD, HEAD, 1)
        value_cols = lax.dynamic_slice_in_dim(values, kv_index * HEAD, HEAD, 1)

        def row_step(carry, block_index):
            key_total, value_total = carry
            start = (block_index * block).astype(jnp.int32)
            row_pos = lax.dynamic_slice_in_dim(positions, start, block)
            visible = positions[None, :] <= row_pos[:, None]
            pieces = []
            for member in range(members):
                head_id = (kv_index * members + member).astype(jnp.int32)
                query_all = lax.dynamic_slice_in_dim(queries, head_id * HEAD, HEAD, 1)
                grad_all = lax.dynamic_slice_in_dim(out_grad, head_id * HEAD, HEAD, 1)
                query_cols = lax.dynamic_slice_in_dim(query_all, start, block, 0)
                grad_cols = lax.dynamic_slice_in_dim(grad_all, start, block, 0)
                scores = jnp.dot(query_cols, key_cols.T, preferred_element_type=jnp.float32) * factor
                scores = jnp.where(visible, scores, jnp.float32(-1e+30))
                top_score = lax.optimization_barrier(jnp.max(scores, axis=1, keepdims=True))
                log_total = top_score + jnp.log(lax.optimization_barrier(jnp.sum(jnp.exp(scores - top_score), axis=1, keepdims=True)))
                weights = jnp.exp(scores - log_total)
                value_total = value_total + jnp.dot(weights.astype(jnp.bfloat16).T, grad_cols, preferred_element_type=jnp.float32)
                dweight = jnp.dot(grad_cols, value_cols.T, preferred_element_type=jnp.float32)
                delta_col = lax.dynamic_slice_in_dim(delta, head_id, 1, 1)
                row_delta = lax.dynamic_slice_in_dim(delta_col, start, block, 0)
                dscore = (weights * (dweight - row_delta) * factor).astype(jnp.bfloat16)
                pieces.append(jnp.dot(dscore, key_cols, preferred_element_type=jnp.float32))
                key_total = key_total + jnp.dot(dscore.T, query_cols, preferred_element_type=jnp.float32)
            return ((key_total, value_total), jnp.concatenate(pieces, axis=1))
        start_carry = (jnp.zeros((TOKENS, HEAD), jnp.float32), jnp.zeros((TOKENS, HEAD), jnp.float32))
        totals, query_rows = lax.scan(row_step, start_carry, jnp.arange(blocks, dtype=jnp.int32))
        return (query_rows.reshape(TOKENS, members * HEAD), totals[0], totals[1])
    query_parts, key_parts, value_parts = lax.map(one_group, jnp.arange(KV_HEADS, dtype=jnp.int32))
    query_grad = jnp.transpose(query_parts, (1, 0, 2)).reshape(TOKENS, HEADS * HEAD).astype(jnp.bfloat16)
    key_grad = jnp.transpose(key_parts, (1, 0, 2)).reshape(TOKENS, KV_HEADS * HEAD).astype(jnp.bfloat16)
    value_grad = jnp.transpose(value_parts, (1, 0, 2)).reshape(TOKENS, KV_HEADS * HEAD).astype(jnp.bfloat16)
    return (query_grad, key_grad, value_grad)
```

```python
import functools
import math

import jax
import jax.numpy as jnp
from jax import lax
from jax.experimental import pallas as pl
from jax.experimental.pallas import tpu as pltpu
from jax.sharding import PartitionSpec as P

HEADS = 16
KV_HEADS = 4
HEAD = 64
STRETCH = 64
MEMBERS = HEADS // KV_HEADS
LANES = MEMBERS * STRETCH
KB = 512


def attention_kernel(
    key_at, query_at, q_ref, g_ref, o_ref, kv_ref, dq_ref, dkv_ref,
    kvs, kts, scr, acc, xq_t, xg_t, xq, xg,
):
    tokens = kv_ref.shape[0]
    stretches = tokens // STRETCH
    f32, bf16 = jnp.float32, jnp.bfloat16
    lane = lax.broadcasted_iota(jnp.int32, (1, 2 * HEAD), 1)
    scale = jnp.where(lane < HEAD, 0.125, 1.0).astype(f32)

    def place(t, c):
        src = pl.multiple_of(t * STRETCH, STRETCH)
        dst = pl.multiple_of(key_at[t] * STRETCH, STRETCH)
        kvs[pl.ds(dst, STRETCH), :] = (kv_ref[pl.ds(src, STRETCH), :].astype(f32) * scale).astype(bf16)
        return c

    lax.fori_loop(0, stretches, place, 0)

    def turn(j, c):
        rows = pl.multiple_of(j * KB, KB)
        kts[j] = jnp.transpose(kvs[pl.ds(rows, KB), :])[HEAD:, :]
        acc[pl.ds(rows, KB), :] = jnp.zeros((KB, 2 * HEAD), f32)
        return c

    lax.fori_loop(0, tokens // KB, turn, 0)

    def by_head(block):
        flat = jnp.transpose(block.astype(f32))
        return jnp.concatenate([flat[h * HEAD : (h + 1) * HEAD] for h in range(MEMBERS)], axis=1)

    def one_stretch(st, c):
        rows = pl.multiple_of(st * STRETCH, STRETCH)
        at = query_at[st]
        q_t = by_head(q_ref[pl.ds(rows, STRETCH), :]) * 0.125
        g_t = by_head(g_ref[pl.ds(rows, STRETCH), :])
        o_t = by_head(o_ref[pl.ds(rows, STRETCH), :])
        delta = jnp.sum(g_t * o_t, axis=0, keepdims=True) * 0.125
        zero_t = jnp.zeros((HEAD, LANES), f32)
        q_pad = jnp.concatenate([zero_t, q_t], axis=0)
        g_pad = jnp.concatenate([g_t, zero_t], axis=0)
        xq_t[...] = q_pad.astype(bf16)
        xg_t[...] = g_pad.astype(bf16)
        xq[...] = jnp.transpose(q_pad).astype(bf16)
        xg[...] = jnp.transpose(g_pad).astype(bf16)
        full = (at * STRETCH) // KB

        def scores(j):
            kr = pl.multiple_of(j * KB, KB)
            return kr, jnp.dot(kvs[pl.ds(kr, KB), :], xq_t[...], preferred_element_type=f32)

        def fold_max(s, m):
            return jnp.maximum(m, jnp.max(s.reshape(KB // 8, 8, LANES), axis=0))

        def first(j, m):
            kr, s = scores(j)
            scr[pl.ds(kr, KB), :] = s
            return fold_max(s, m)

        m = lax.fori_loop(0, full, first, jnp.full((8, LANES), -1e30, f32))
        kr, s = scores(full)
        key_pos = kr + lax.broadcasted_iota(jnp.int32, (KB, LANES), 0)
        row_pos = at * STRETCH + lax.rem(lax.broadcasted_iota(jnp.int32, (KB, LANES), 1), STRETCH)
        s = jnp.where(key_pos <= row_pos, s, -1e30)
        scr[pl.ds(kr, KB), :] = s
        m = jnp.max(fold_max(s, m), axis=0, keepdims=True)

        def second(j, total):
            kr = pl.multiple_of(j * KB, KB)
            e = jnp.exp(scr[pl.ds(kr, KB), :] - m)
            scr[pl.ds(kr, KB), :] = e
            return total + jnp.sum(e.reshape(KB // 8, 8, LANES), axis=0)

        total = lax.fori_loop(0, full + 1, second, jnp.zeros((8, LANES), f32))
        inverse = 1.0 / jnp.sum(total, axis=0, keepdims=True)

        def third(j, dq):
            kr = pl.multiple_of(j * KB, KB)
            w = scr[pl.ds(kr, KB), :] * inverse
            dw = jnp.dot(kvs[pl.ds(kr, KB), :], xg_t[...], preferred_element_type=f32)
            ds = (w * (dw - delta)).astype(bf16)
            acc[pl.ds(kr, KB), :] += jnp.dot(
                w.astype(bf16), xg[...], preferred_element_type=f32
            ) + jnp.dot(ds, xq[...], preferred_element_type=f32)
            return dq + jnp.dot(kts[j], ds, preferred_element_type=f32)

        dq = lax.fori_loop(0, full + 1, third, jnp.zeros((HEAD, LANES), f32))
        flat = jnp.concatenate([dq[:, h * STRETCH : (h + 1) * STRETCH] for h in range(MEMBERS)], axis=0)
        dq_ref[pl.ds(rows, STRETCH), :] = jnp.transpose(flat).astype(bf16)
        return c

    lax.fori_loop(0, q_ref.shape[0] // STRETCH, one_stretch, 0)
    gain = jnp.where(lane < HEAD, 1.0, 8.0).astype(f32)

    def restore(t, c):
        dst = pl.multiple_of(t * STRETCH, STRETCH)
        src = pl.multiple_of(key_at[t] * STRETCH, STRETCH)
        dkv_ref[pl.ds(dst, STRETCH), :] = (acc[pl.ds(src, STRETCH), :] * gain).astype(dkv_ref.dtype)
        return c

    lax.fori_loop(0, stretches, restore, 0)


def attention(key_at, query_at, q, g, o, kv, out_type):
    tokens = kv.shape[0]
    vmem = pl.BlockSpec(memory_space=pltpu.VMEM)
    smem = pl.BlockSpec(memory_space=pltpu.SMEM)
    return pl.pallas_call(
        attention_kernel,
        out_shape=(
            jax.ShapeDtypeStruct(q.shape, jnp.bfloat16),
            jax.ShapeDtypeStruct((tokens, 2 * HEAD), out_type),
        ),
        in_specs=[smem, smem, vmem, vmem, vmem, vmem],
        out_specs=(vmem, vmem),
        scratch_shapes=[
            pltpu.VMEM((tokens, 2 * HEAD), jnp.bfloat16),
            pltpu.VMEM((tokens // KB, HEAD, KB), jnp.bfloat16),
            pltpu.VMEM((tokens, LANES), jnp.float32),
            pltpu.VMEM((tokens, 2 * HEAD), jnp.float32),
            pltpu.VMEM((2 * HEAD, LANES), jnp.bfloat16),
            pltpu.VMEM((2 * HEAD, LANES), jnp.bfloat16),
            pltpu.VMEM((LANES, 2 * HEAD), jnp.bfloat16),
            pltpu.VMEM((LANES, 2 * HEAD), jnp.bfloat16),
        ],
        compiler_params=pltpu.CompilerParams(vmem_limit_bytes=52 * 1024 * 1024),
    )(key_at, query_at, q, g, o, kv)


def per_device(queries, keys, values, outputs, out_grad, positions):
    rows = queries.shape[0]
    ranks = lax.axis_size("qrow")
    cols = lax.axis_size("kcol")
    halves = cols // KV_HEADS
    part = rows // halves
    mine = lax.axis_index("qrow")
    half = lax.rem(lax.axis_index("kcol"), halves)
    key_at = positions.reshape(-1, STRETCH)[:, 0] // STRETCH
    query_at = lax.dynamic_slice(
        key_at.reshape(cols, ranks, halves, part // STRETCH),
        (0, mine, half, 0),
        (cols, 1, 1, part // STRETCH),
    ).reshape(-1)

    def by_query(x):
        x = x.reshape(halves, part, KV_HEADS, LANES).transpose(2, 0, 1, 3)
        x = lax.all_to_all(x.reshape(cols, part, LANES), "kcol", 0, 0)
        return x.reshape(cols * part, LANES)

    def by_key(x):
        x = x.reshape(rows, KV_HEADS, 1, HEAD).transpose(1, 2, 0, 3)
        x = jnp.broadcast_to(x, (KV_HEADS, halves, rows, HEAD)).reshape(cols, rows, HEAD)
        return lax.all_to_all(x, "kcol", 0, 0).reshape(cols * rows, HEAD)

    q, g, o = by_query(queries), by_query(out_grad), by_query(outputs)
    own = jnp.concatenate([by_key(values), by_key(keys)], axis=1)
    kv = lax.all_gather(own, "qrow", axis=0, tiled=True)
    dq, dkv = attention(key_at, query_at, q, g, o, kv, jnp.float32)
    dq = lax.all_to_all(dq.reshape(cols, part, LANES), "kcol", 0, 0)
    query_grad = (
        dq.reshape(KV_HEADS, halves, part, LANES).transpose(1, 2, 0, 3).reshape(rows, HEADS * HEAD)
    )
    share = lax.psum_scatter(dkv, "qrow", scatter_dimension=0, tiled=True)
    if halves == 1:
        share = share.astype(jnp.bfloat16)

    def home(x):
        x = lax.all_to_all(x.reshape(cols, rows, HEAD), "kcol", 0, 0)
        x = x.reshape(KV_HEADS, halves, rows, HEAD).sum(1).astype(jnp.bfloat16)
        return x.transpose(1, 0, 2).reshape(rows, KV_HEADS * HEAD)

    return (query_grad, home(share[:, HEAD:]), home(share[:, :HEAD]))


def solution(mesh):
    in_specs = (
        P(("kcol", "qrow"), None),
        P(("qrow", "kcol"), None),
        P(("qrow", "kcol"), None),
        P(("kcol", "qrow"), None),
        P(("kcol", "qrow"), None),
        P(),
    )
    out_specs = (P(("kcol", "qrow"), None), P(("qrow", "kcol"), None), P(("qrow", "kcol"), None))
    return jax.shard_map(
        per_device, mesh=mesh, in_specs=in_specs, out_specs=out_specs, check_vma=False
    )
```

```python
import functools

import jax
import jax.numpy as jnp
from jax import lax
from jax.experimental import pallas as pl
from jax.experimental.pallas import tpu as pltpu
from jax.sharding import PartitionSpec as P

HEADS = 16
KV_HEADS = 4
HEAD = 64
STRETCH = 64
MEMBERS = HEADS // KV_HEADS
LANES = MEMBERS * STRETCH
KB = 512


def attention_kernel(
    key_at, query_at, q_ref, g_ref, d_ref, kv_ref, dq_ref, dkv_ref,
    kvs, kts, scr, acc, xq_t, xg_t, xq, xg,
):
    tokens = kv_ref.shape[0]
    stretches = tokens // STRETCH
    f32, bf16 = jnp.float32, jnp.bfloat16
    lane = lax.broadcasted_iota(jnp.int32, (1, 2 * HEAD), 1)
    each = q_ref.shape[0] // STRETCH // d_ref.shape[0]

    def place(t, c):
        src = pl.multiple_of(t * STRETCH, STRETCH)
        dst = pl.multiple_of(key_at[t] * STRETCH, STRETCH)
        kvs[pl.ds(dst, STRETCH), :] = kv_ref[pl.ds(src, STRETCH), :]
        return c

    lax.fori_loop(0, stretches, place, 0)

    def turn(j, c):
        rows = pl.multiple_of(j * KB, KB)
        kts[j] = jnp.transpose(kvs[pl.ds(rows, KB), :])[HEAD:, :]
        acc[pl.ds(rows, KB), :] = jnp.zeros((KB, 2 * HEAD), f32)
        return c

    lax.fori_loop(0, tokens // KB, turn, 0)

    def by_head(block):
        flat = jnp.transpose(block.astype(f32))
        return jnp.concatenate([flat[h * HEAD : (h + 1) * HEAD] for h in range(MEMBERS)], axis=1)

    def one_stretch(st, c):
        rows = pl.multiple_of(st * STRETCH, STRETCH)
        at = query_at[st]
        q_t = by_head(q_ref[pl.ds(rows, STRETCH), :]) * 0.125
        g_t = by_head(g_ref[pl.ds(rows, STRETCH), :])
        delta = d_ref[st // each, pl.ds(lax.rem(st, each), 1), :]
        zero_t = jnp.zeros((HEAD, LANES), f32)
        q_pad = jnp.concatenate([zero_t, q_t], axis=0)
        g_pad = jnp.concatenate([g_t, zero_t], axis=0)
        xq_t[...] = q_pad.astype(bf16)
        xg_t[...] = g_pad.astype(bf16)
        xq[...] = jnp.transpose(q_pad).astype(bf16)
        xg[...] = jnp.transpose(g_pad).astype(bf16)
        full = (at * STRETCH) // KB

        def scores(j):
            kr = pl.multiple_of(j * KB, KB)
            return kr, jnp.dot(kvs[pl.ds(kr, KB), :], xq_t[...], preferred_element_type=f32)

        def fold_max(s, m):
            return jnp.maximum(m, jnp.max(s.reshape(KB // 8, 8, LANES), axis=0))

        def first(j, m):
            kr, s = scores(j)
            scr[pl.ds(kr, KB), :] = s
            return fold_max(s, m)

        m = lax.fori_loop(0, full, first, jnp.full((8, LANES), -1e30, f32))
        kr, s = scores(full)
        key_pos = kr + lax.broadcasted_iota(jnp.int32, (KB, LANES), 0)
        row_pos = at * STRETCH + lax.rem(lax.broadcasted_iota(jnp.int32, (KB, LANES), 1), STRETCH)
        s = jnp.where(key_pos <= row_pos, s, -1e30)
        scr[pl.ds(kr, KB), :] = s
        m = jnp.max(fold_max(s, m), axis=0, keepdims=True)

        def second(j, total):
            kr = pl.multiple_of(j * KB, KB)
            e = jnp.exp(scr[pl.ds(kr, KB), :] - m)
            scr[pl.ds(kr, KB), :] = e
            return total + jnp.sum(e.reshape(KB // 8, 8, LANES), axis=0)

        total = lax.fori_loop(0, full + 1, second, jnp.zeros((8, LANES), f32))
        inverse = 1.0 / jnp.sum(total, axis=0, keepdims=True)

        def third(j, dq):
            kr = pl.multiple_of(j * KB, KB)
            w = scr[pl.ds(kr, KB), :] * inverse
            dw = jnp.dot(kvs[pl.ds(kr, KB), :], xg_t[...], preferred_element_type=f32)
            ds = (w * (dw - delta)).astype(bf16)
            acc[pl.ds(kr, KB), :] += jnp.dot(
                w.astype(bf16), xg[...], preferred_element_type=f32
            ) + jnp.dot(ds, xq[...], preferred_element_type=f32)
            return dq + jnp.dot(kts[j], ds, preferred_element_type=f32)

        dq = lax.fori_loop(0, full + 1, third, jnp.zeros((HEAD, LANES), f32))
        flat = jnp.concatenate([dq[:, h * STRETCH : (h + 1) * STRETCH] for h in range(MEMBERS)], axis=0)
        dq_ref[pl.ds(rows, STRETCH), :] = jnp.transpose(flat).astype(bf16)
        return c

    lax.fori_loop(0, q_ref.shape[0] // STRETCH, one_stretch, 0)
    gain = jnp.where(lane < HEAD, 1.0, 8.0).astype(f32)

    def restore(t, c):
        dst = pl.multiple_of(t * STRETCH, STRETCH)
        src = pl.multiple_of(key_at[t] * STRETCH, STRETCH)
        dkv_ref[pl.ds(dst, STRETCH), :] = (acc[pl.ds(src, STRETCH), :] * gain).astype(dkv_ref.dtype)
        return c

    lax.fori_loop(0, stretches, restore, 0)


def attention(key_at, query_at, q, g, d, kv, out_type):
    tokens = kv.shape[0]
    vmem = pl.BlockSpec(memory_space=pltpu.VMEM)
    smem = pl.BlockSpec(memory_space=pltpu.SMEM)
    return pl.pallas_call(
        attention_kernel,
        out_shape=(
            jax.ShapeDtypeStruct(q.shape, jnp.bfloat16),
            jax.ShapeDtypeStruct((tokens, 2 * HEAD), out_type),
        ),
        in_specs=[smem, smem, vmem, vmem, vmem, vmem],
        out_specs=(vmem, vmem),
        scratch_shapes=[
            pltpu.VMEM((tokens, 2 * HEAD), jnp.bfloat16),
            pltpu.VMEM((tokens // KB, HEAD, KB), jnp.bfloat16),
            pltpu.VMEM((tokens, LANES), jnp.float32),
            pltpu.VMEM((tokens, 2 * HEAD), jnp.float32),
            pltpu.VMEM((2 * HEAD, LANES), jnp.bfloat16),
            pltpu.VMEM((2 * HEAD, LANES), jnp.bfloat16),
            pltpu.VMEM((LANES, 2 * HEAD), jnp.bfloat16),
            pltpu.VMEM((LANES, 2 * HEAD), jnp.bfloat16),
        ],
        compiler_params=pltpu.CompilerParams(vmem_limit_bytes=52 * 1024 * 1024),
    )(key_at, query_at, q, g, d, kv)


def greet(ranks, cols):
    r, c = lax.axis_index("qrow"), lax.axis_index("kcol")
    barrier = pltpu.get_barrier_semaphore()
    count = 0
    for k in range(1, cols):
        signal(barrier, (r, lax.rem(c + k, cols)))
        count += 1
    for k in range(1, ranks // 2):
        signal(barrier, (lax.rem(r + 2 * k, ranks), c))
        count += 1
    signal(barrier, (r + 1 - 2 * lax.rem(r, 2), c))
    pl.semaphore_wait(barrier, count + 1)


def signal(semaphore, device):
    pl.semaphore_signal(
        semaphore, inc=1, device_id=device, device_id_type=pl.DeviceIdType.MESH
    )


def remote(src, dst, send, recv, device):
    return pltpu.make_async_remote_copy(
        src_ref=src, dst_ref=dst, send_sem=send, recv_sem=recv,
        device_id=device, device_id_type=pl.DeviceIdType.MESH,
    )


def gather_kernel(
    ranks, cols, q_ref, g_ref, o_ref, k_ref, v_ref, q_out, g_out, d_out, kv_out,
    packed, terms, send_a, recv_a, send_z, recv_z, send_s, recv_s,
):
    f32, bf16 = jnp.float32, jnp.bfloat16
    r, c = lax.axis_index("qrow"), lax.axis_index("kcol")
    sibling = r + 1 - 2 * lax.rem(r, 2)
    rows = q_ref.shape[0]
    halves = cols // KV_HEADS
    part = rows // halves
    block = cols * rows
    greet(ranks, cols)

    def key_rows(rank, col):
        return pl.ds(pl.multiple_of((rank * cols + col) * rows, rows), rows)

    def query_rows(col):
        return pl.ds(pl.multiple_of(col * part, part), part)

    def query_slice(col):
        half = pl.ds(pl.multiple_of(lax.rem(col, halves) * part, part), part)
        return half, pl.ds(pl.multiple_of((col // halves) * LANES, LANES), LANES)

    for h in range(KV_HEADS):
        cut = slice(h * HEAD, (h + 1) * HEAD)
        packed[h] = jnp.concatenate(
            [(v_ref[:, cut].astype(f32) * 0.125).astype(bf16), k_ref[:, cut]], axis=1
        )

    def to_peer(k, which, src, dst, peer):
        return remote(src, dst, send_a.at[k, which], recv_a.at[k, which], (r, peer))

    copies = []
    for k in range(1, cols):
        peer = lax.rem(c + k, cols)
        copies.append(
            to_peer(k, 0, packed.at[peer // halves], kv_out.at[key_rows(r, c)], peer)
        )
        copies[-1].start()
    for k in range(1, cols):
        peer = lax.rem(c + k, cols)
        for which, (src, dst) in enumerate([(q_ref, q_out), (g_ref, g_out)]):
            half, columns = query_slice(peer)
            copies.append(
                to_peer(k, 1 + which, src.at[half, columns], dst.at[query_rows(c)], peer)
            )
            copies[-1].start()
    kv_out[key_rows(r, c), :] = packed[c // halves]
    half, columns = query_slice(c)
    q_out[query_rows(c), :] = q_ref[half, columns]
    g_out[query_rows(c), :] = g_ref[half, columns]

    for h in range(KV_HEADS):
        cut = slice(h * LANES, (h + 1) * LANES)
        product = jnp.transpose(g_ref[:, cut].astype(f32) * o_ref[:, cut].astype(f32))
        sums = jnp.sum(product.reshape(MEMBERS, HEAD, rows), axis=1) * 0.125
        for u in range(rows // STRETCH):
            line = jnp.concatenate(
                [sums[m : m + 1, u * STRETCH : (u + 1) * STRETCH] for m in range(MEMBERS)], axis=1
            )
            each = part // STRETCH
            terms[h * halves + u // each, u % each : u % each + 1, :] = line
    for k in range(1, cols):
        peer = lax.rem(c + k, cols)
        copies.append(to_peer(k, 3, terms.at[peer], d_out.at[c], peer))
        copies[-1].start()
    d_out[c] = terms[c]

    def from_peer(k, which, dst):
        return remote(dst, dst, send_a.at[k, which], recv_a.at[k, which], (r, lax.rem(c + k, cols)))

    for k in range(1, cols):
        source = lax.rem(c + cols - k, cols)
        from_peer(k, 0, kv_out.at[key_rows(r, source)]).wait_recv()

    def whole(rank):
        return kv_out.at[pl.ds(pl.multiple_of(rank * block, block), block)]

    for k in range(1, ranks // 2):
        peer = lax.rem(r + 2 * k, ranks)
        copies.append(remote(whole(r), whole(r), send_z.at[k], recv_z.at[k], (peer, c)))
        copies[-1].start()
    copies.append(remote(whole(r), whole(r), send_s.at[0], recv_s.at[0], (sibling, c)))
    copies[-1].start()
    for k in range(1, ranks // 2):
        source = lax.rem(r + ranks - 2 * k, ranks)
        peer = lax.rem(r + 2 * k, ranks)
        here = whole(source)
        remote(here, here, send_z.at[k], recv_z.at[k], (peer, c)).wait_recv()
        copies.append(remote(here, here, send_s.at[k], recv_s.at[k], (sibling, c)))
        copies[-1].start()
    for k in range(ranks // 2):
        here = whole(lax.rem(sibling + ranks - 2 * k, ranks))
        remote(here, here, send_s.at[k], recv_s.at[k], (sibling, c)).wait_recv()
    for k in range(1, cols):
        source = lax.rem(c + cols - k, cols)
        from_peer(k, 1, q_out.at[query_rows(source)]).wait_recv()
        from_peer(k, 2, g_out.at[query_rows(source)]).wait_recv()
        from_peer(k, 3, d_out.at[source]).wait_recv()
    for copy in copies:
        copy.wait_send()


def gather(queries, out_grad, outputs, keys, values, ranks, cols):
    rows = queries.shape[0]
    part = rows // (cols // KV_HEADS)
    bf16 = jnp.bfloat16
    vmem = pl.BlockSpec(memory_space=pltpu.VMEM)
    dma = pltpu.SemaphoreType.DMA
    return pl.pallas_call(
        functools.partial(gather_kernel, ranks, cols),
        out_shape=(
            jax.ShapeDtypeStruct((cols * part, LANES), bf16),
            jax.ShapeDtypeStruct((cols * part, LANES), bf16),
            jax.ShapeDtypeStruct((cols, 8, LANES), jnp.float32),
            jax.ShapeDtypeStruct((ranks * cols * rows, 2 * HEAD), bf16),
        ),
        in_specs=[vmem] * 5,
        out_specs=(vmem,) * 4,
        scratch_shapes=[
            pltpu.VMEM((KV_HEADS, rows, 2 * HEAD), bf16),
            pltpu.VMEM((cols, 8, LANES), jnp.float32),
            dma((cols, 4)), dma((cols, 4)),
            dma((ranks // 2,)), dma((ranks // 2,)),
            dma((ranks // 2,)), dma((ranks // 2,)),
        ],
        compiler_params=pltpu.CompilerParams(
            collective_id=0, has_side_effects=True, vmem_limit_bytes=40 * 1024 * 1024
        ),
    )(queries, out_grad, outputs, keys, values)


def scatter_kernel(
    ranks, cols, dq_ref, dkv_ref, q_out, k_out, v_out,
    near, passing, far, share, last,
    send_q, recv_q, send_s, recv_s, send_z, recv_z, send_a, recv_a,
):
    f32, bf16 = jnp.float32, jnp.bfloat16
    r, c = lax.axis_index("qrow"), lax.axis_index("kcol")
    sibling = r + 1 - 2 * lax.rem(r, 2)
    rows = q_out.shape[0]
    halves = cols // KV_HEADS
    part = rows // halves
    block = cols * rows
    steps = ranks // 2
    greet(ranks, cols)

    def span(rank):
        return pl.ds(pl.multiple_of(rank * block, block), block)

    def query_rows(col):
        return pl.ds(pl.multiple_of(col * part, part), part)

    def query_slice(col):
        half = pl.ds(pl.multiple_of(lax.rem(col, halves) * part, part), part)
        return half, pl.ds(pl.multiple_of((col // halves) * LANES, LANES), LANES)

    copies = []
    order = list(range(1, steps)) + [0]
    for k in order:
        target = lax.rem(sibling + 2 * k, ranks)
        copies.append(
            remote(dkv_ref.at[span(target)], near.at[k], send_s.at[k], recv_s.at[k], (sibling, c))
        )
        copies[-1].start()
    for k in order:
        peer = lax.rem(r + 2 * k, ranks)
        remote(near.at[k], near.at[k], send_s.at[k], recv_s.at[k], (sibling, c)).wait_recv()
        both = dkv_ref[span(peer), :].astype(f32) + near[k].astype(f32)
        if k:
            passing[k] = both.astype(bf16)
            copies.append(
                remote(passing.at[k], far.at[k], send_z.at[k], recv_z.at[k], (peer, c))
            )
            copies[-1].start()
    half, columns = query_slice(c)
    for k in range(1, cols):
        peer = lax.rem(c + k, cols)
        copies.append(
            remote(
                dq_ref.at[query_rows(peer)], q_out.at[half, columns],
                send_q.at[k], recv_q.at[k], (r, peer),
            )
        )
        copies[-1].start()
    q_out[half, columns] = dq_ref[query_rows(c), :]
    total = both
    for k in range(1, steps):
        peer = lax.rem(r + 2 * k, ranks)
        remote(far.at[k], far.at[k], send_z.at[k], recv_z.at[k], (peer, c)).wait_recv()
        total = total + far[k].astype(f32)
    share[...] = total.astype(bf16)

    def share_rows(col):
        return pl.ds(pl.multiple_of(col * rows, rows), rows)

    for k in range(1, cols):
        peer = lax.rem(c + k, cols)
        copies.append(
            remote(share.at[share_rows(peer)], last.at[c], send_a.at[k], recv_a.at[k], (r, peer))
        )
        copies[-1].start()
    last[c] = share[share_rows(c), :]
    for k in range(1, cols):
        peer = lax.rem(c + k, cols)
        here = last.at[lax.rem(c + cols - k, cols)]
        remote(here, here, send_a.at[k], recv_a.at[k], (r, peer)).wait_recv()
    k_parts, v_parts = [], []
    for h in range(KV_HEADS):
        whole = last[h * halves].astype(f32)
        for other in range(1, halves):
            whole = whole + last[h * halves + other].astype(f32)
        v_parts.append(whole[:, :HEAD])
        k_parts.append(whole[:, HEAD:])
    k_out[...] = jnp.concatenate(k_parts, axis=1).astype(bf16)
    v_out[...] = jnp.concatenate(v_parts, axis=1).astype(bf16)
    for k in range(1, cols):
        peer = lax.rem(c + k, cols)
        half, columns = query_slice(lax.rem(c + cols - k, cols))
        here = q_out.at[half, columns]
        remote(dq_ref.at[query_rows(peer)], here, send_q.at[k], recv_q.at[k], (r, peer)).wait_recv()
    for copy in copies:
        copy.wait_send()


def scatter(dq, dkv, rows, ranks, cols):
    bf16 = jnp.bfloat16
    vmem = pl.BlockSpec(memory_space=pltpu.VMEM)
    dma = pltpu.SemaphoreType.DMA
    block = cols * rows
    return pl.pallas_call(
        functools.partial(scatter_kernel, ranks, cols),
        out_shape=(
            jax.ShapeDtypeStruct((rows, HEADS * HEAD), bf16),
            jax.ShapeDtypeStruct((rows, KV_HEADS * HEAD), bf16),
            jax.ShapeDtypeStruct((rows, KV_HEADS * HEAD), bf16),
        ),
        in_specs=[vmem] * 2,
        out_specs=(vmem,) * 3,
        scratch_shapes=[
            pltpu.VMEM((ranks // 2, block, 2 * HEAD), bf16),
            pltpu.VMEM((ranks // 2, block, 2 * HEAD), bf16),
            pltpu.VMEM((ranks // 2, block, 2 * HEAD), bf16),
            pltpu.VMEM((block, 2 * HEAD), bf16),
            pltpu.VMEM((cols, rows, 2 * HEAD), bf16),
            dma((cols,)), dma((cols,)),
            dma((ranks // 2,)), dma((ranks // 2,)),
            dma((ranks // 2,)), dma((ranks // 2,)),
            dma((cols,)), dma((cols,)),
        ],
        compiler_params=pltpu.CompilerParams(
            collective_id=1, has_side_effects=True, vmem_limit_bytes=40 * 1024 * 1024
        ),
    )(dq, dkv)


def per_device(queries, keys, values, outputs, out_grad, positions):
    rows = queries.shape[0]
    ranks = lax.axis_size("qrow")
    cols = lax.axis_size("kcol")
    halves = cols // KV_HEADS
    each = rows // halves // STRETCH
    mine = lax.axis_index("qrow")
    half = lax.rem(lax.axis_index("kcol"), halves)
    key_at = positions.reshape(-1, STRETCH)[:, 0] // STRETCH
    query_at = lax.dynamic_slice(
        key_at.reshape(cols, ranks, halves, each), (0, mine, half, 0), (cols, 1, 1, each)
    ).reshape(-1)
    q, g, d, kv = gather(queries, out_grad, outputs, keys, values, ranks, cols)
    dq, dkv = attention(key_at, query_at, q, g, d, kv, jnp.bfloat16)
    return scatter(dq, dkv, rows, ranks, cols)


def solution(mesh):
    in_specs = (
        P(("kcol", "qrow"), None),
        P(("qrow", "kcol"), None),
        P(("qrow", "kcol"), None),
        P(("kcol", "qrow"), None),
        P(("kcol", "qrow"), None),
        P(),
    )
    out_specs = (P(("kcol", "qrow"), None), P(("qrow", "kcol"), None), P(("qrow", "kcol"), None))
    return jax.shard_map(
        per_device, mesh=mesh, in_specs=in_specs, out_specs=out_specs, check_vma=False
    )
```

```python
import functools

import jax
import jax.numpy as jnp
from jax import lax
from jax.experimental import pallas as pl
from jax.experimental.pallas import tpu as pltpu
from jax.sharding import PartitionSpec as P

HEADS = 16
KV_HEADS = 4
HEAD = 64
STRETCH = 64
MEMBERS = HEADS // KV_HEADS
LANES = MEMBERS * STRETCH
KB = 1024


def attention_kernel(
    ranks, cols, positions, q_ref, g_ref, d_ref, kv_ref, dq_ref, dkv_ref,
    kvs, kts, scr, acc, xq_t, xg_t, xx,
):
    tokens = kv_ref.shape[0]
    stretches = tokens // STRETCH
    f32, bf16 = jnp.float32, jnp.bfloat16
    rows = tokens // (ranks * cols)
    halves = cols // KV_HEADS
    part = rows // halves
    each = part // STRETCH
    rank = lax.axis_index("qrow")
    half = lax.rem(lax.axis_index("kcol"), halves)
    lane = lax.broadcasted_iota(jnp.int32, (1, 2 * HEAD), 1)

    def place(t, c):
        src = pl.multiple_of(t * STRETCH, STRETCH)
        dst = pl.multiple_of(positions[src], STRETCH)
        kvs[pl.ds(dst, STRETCH), :] = kv_ref[pl.ds(src, STRETCH), :]
        return c

    lax.fori_loop(0, stretches, place, 0, unroll=8)

    def turn(j, c):
        at = pl.multiple_of(j * KB, KB)
        kts[j] = jnp.transpose(kvs[pl.ds(at, KB), :])[HEAD:, :]
        acc[pl.ds(at, KB), :] = jnp.zeros((KB, 2 * HEAD), f32)
        return c

    lax.fori_loop(0, tokens // KB, turn, 0)

    def head_rows(block, upper):
        pieces = []
        for h in range(MEMBERS):
            pair = block[:, (h // 2) * 2 * HEAD : (h // 2 + 1) * 2 * HEAD]
            if (h % 2 == 1) != upper:
                pair = pltpu.roll(pair, HEAD, 1)
            pieces.append(jnp.where((lane >= HEAD) == upper, pair, 0.0))
        return jnp.concatenate(pieces, axis=0)

    def one_stretch(st, c):
        at = pl.multiple_of(st * STRETCH, STRETCH)
        origin = ((st // each) * ranks + rank) * rows + half * part + lax.rem(st, each) * STRETCH
        start = positions[origin]
        g_rows = head_rows(g_ref[pl.ds(at, STRETCH), :].astype(f32), False)
        q_rows = head_rows(q_ref[pl.ds(at, STRETCH), :].astype(f32) * 0.125, True)
        delta = d_ref[st // each, pl.ds(lax.rem(st, each), 1), :]
        xx[:LANES] = g_rows.astype(bf16)
        xx[LANES:] = q_rows.astype(bf16)
        turned = jnp.transpose(g_rows + q_rows).astype(bf16)
        none = jnp.zeros((HEAD, LANES), bf16)
        xg_t[:HEAD] = turned[:HEAD]
        xg_t[HEAD:] = none
        xq_t[:HEAD] = none
        xq_t[HEAD:] = turned[HEAD:]
        full = start // KB

        def scores(j):
            kr = pl.multiple_of(j * KB, KB)
            return kr, jnp.dot(kvs[pl.ds(kr, KB), :], xq_t[...], preferred_element_type=f32)

        def fold_max(s, m):
            return jnp.maximum(m, jnp.max(s.reshape(KB // 8, 8, LANES), axis=0))

        def first(j, m):
            kr, s = scores(j)
            scr[pl.ds(kr, KB), :] = s
            return fold_max(s, m)

        m = lax.fori_loop(0, full, first, jnp.full((8, LANES), -1e30, f32))
        kr, s = scores(full)
        key_pos = kr - start + lax.broadcasted_iota(jnp.int32, (KB, LANES), 0)
        row_pos = lax.rem(lax.broadcasted_iota(jnp.int32, (1, LANES), 1), STRETCH)
        s = jnp.where(key_pos <= row_pos, s, -1e30)
        scr[pl.ds(kr, KB), :] = s
        m = jnp.max(fold_max(s, m), axis=0, keepdims=True)

        def second(j, total):
            kr = pl.multiple_of(j * KB, KB)
            e = jnp.exp(scr[pl.ds(kr, KB), :] - m)
            scr[pl.ds(kr, KB), :] = e
            return total + jnp.sum(e.reshape(KB // 8, 8, LANES), axis=0)

        total = lax.fori_loop(0, full + 1, second, jnp.zeros((8, LANES), f32))
        inverse = 1.0 / jnp.sum(total, axis=0, keepdims=True)

        def third(j, dq):
            kr = pl.multiple_of(j * KB, KB)
            w = scr[pl.ds(kr, KB), :] * inverse
            dw = jnp.dot(kvs[pl.ds(kr, KB), :], xg_t[...], preferred_element_type=f32)
            ds = (w * (dw - delta)).astype(bf16)
            both = jnp.concatenate([w.astype(bf16), ds], axis=1)
            acc[pl.ds(kr, KB), :] += jnp.dot(both, xx[...], preferred_element_type=f32)
            return dq + jnp.dot(kts[j], ds, preferred_element_type=f32)

        dq = lax.fori_loop(0, full + 1, third, jnp.zeros((HEAD, LANES), f32))
        flat = jnp.concatenate([dq[:, h * STRETCH : (h + 1) * STRETCH] for h in range(MEMBERS)], axis=0)
        dq_ref[pl.ds(at, STRETCH), :] = jnp.transpose(flat).astype(bf16)
        return c

    lax.fori_loop(0, q_ref.shape[0] // STRETCH, one_stretch, 0)
    gain = jnp.where(lane < HEAD, 1.0, 8.0).astype(f32)

    def restore(t, c):
        dst = pl.multiple_of(t * STRETCH, STRETCH)
        src = pl.multiple_of(positions[dst], STRETCH)
        dkv_ref[pl.ds(dst, STRETCH), :] = (acc[pl.ds(src, STRETCH), :] * gain).astype(dkv_ref.dtype)
        return c

    lax.fori_loop(0, stretches, restore, 0, unroll=8)


def attention(positions, q, g, d, kv, ranks, cols):
    tokens = kv.shape[0]
    vmem = pl.BlockSpec(memory_space=pltpu.VMEM)
    smem = pl.BlockSpec(memory_space=pltpu.SMEM)
    bf16, f32 = jnp.bfloat16, jnp.float32
    return pl.pallas_call(
        functools.partial(attention_kernel, ranks, cols),
        out_shape=(
            jax.ShapeDtypeStruct(q.shape, bf16),
            jax.ShapeDtypeStruct((tokens, 2 * HEAD), bf16),
        ),
        in_specs=[smem, vmem, vmem, vmem, vmem],
        out_specs=(vmem, vmem),
        scratch_shapes=[
            pltpu.VMEM((tokens, 2 * HEAD), bf16),
            pltpu.VMEM((tokens // KB, HEAD, KB), bf16),
            pltpu.VMEM((tokens, LANES), f32),
            pltpu.VMEM((tokens, 2 * HEAD), f32),
            pltpu.VMEM((2 * HEAD, LANES), bf16),
            pltpu.VMEM((2 * HEAD, LANES), bf16),
            pltpu.VMEM((2 * LANES, 2 * HEAD), bf16),
        ],
        compiler_params=pltpu.CompilerParams(vmem_limit_bytes=52 * 1024 * 1024),
    )(positions, q, g, d, kv)


def greet(ranks, cols):
    r, c = lax.axis_index("qrow"), lax.axis_index("kcol")
    barrier = pltpu.get_barrier_semaphore()
    count = 0
    for k in range(1, cols):
        signal(barrier, (r, lax.rem(c + k, cols)))
        count += 1
    for k in range(1, ranks // 2):
        signal(barrier, (lax.rem(r + 2 * k, ranks), c))
        count += 1
    signal(barrier, (r + 1 - 2 * lax.rem(r, 2), c))
    pl.semaphore_wait(barrier, count + 1)


def signal(semaphore, device):
    pl.semaphore_signal(
        semaphore, inc=1, device_id=device, device_id_type=pl.DeviceIdType.MESH
    )


def remote(src, dst, send, recv, device):
    return pltpu.make_async_remote_copy(
        src_ref=src, dst_ref=dst, send_sem=send, recv_sem=recv,
        device_id=device, device_id_type=pl.DeviceIdType.MESH,
    )


def gather_kernel(
    ranks, cols, q_any, g_any, o_any, k_any, v_any, q_out, g_out, d_out, kv_out,
    packed, terms, g_ref, o_ref, k_ref, v_ref, fetched, send_a, recv_a, send_z, recv_z, send_s, recv_s,
):
    f32, bf16 = jnp.float32, jnp.bfloat16
    r, c = lax.axis_index("qrow"), lax.axis_index("kcol")
    sibling = r + 1 - 2 * lax.rem(r, 2)
    rows = q_any.shape[0]
    halves = cols // KV_HEADS
    part = rows // halves
    block = cols * rows
    pairs = [(k_any, k_ref), (v_any, v_ref), (g_any, g_ref), (o_any, o_ref)]
    fetches = [pltpu.make_async_copy(a, b, fetched.at[n]) for n, (a, b) in enumerate(pairs)]
    for fetch in fetches:
        fetch.start()

    def key_rows(rank, col):
        return pl.ds(pl.multiple_of((rank * cols + col) * rows, rows), rows)

    def query_rows(col):
        return pl.ds(pl.multiple_of(col * part, part), part)

    def query_slice(col):
        half = pl.ds(pl.multiple_of(lax.rem(col, halves) * part, part), part)
        return half, pl.ds(pl.multiple_of((col // halves) * LANES, LANES), LANES)

    half, columns = query_slice(c)
    own_query = pltpu.make_async_copy(
        q_any.at[half, columns], q_out.at[query_rows(c)], fetched.at[4]
    )
    own_query.start()
    fetches[0].wait()
    fetches[1].wait()
    for h in range(KV_HEADS):
        cut = slice(h * HEAD, (h + 1) * HEAD)
        packed[h] = jnp.concatenate(
            [(v_ref[:, cut].astype(f32) * 0.125).astype(bf16), k_ref[:, cut]], axis=1
        )

    greet(ranks, cols)

    def to_peer(k, which, src, dst, peer):
        return remote(src, dst, send_a.at[k, which], recv_a.at[k, which], (r, peer))

    copies = []
    for k in range(1, cols):
        peer = lax.rem(c + k, cols)
        copies.append(
            to_peer(k, 0, packed.at[peer // halves], kv_out.at[key_rows(r, c)], peer)
        )
        copies[-1].start()
    for k in range(1, cols):
        peer = lax.rem(c + k, cols)
        for which, (src, dst) in enumerate([(q_any, q_out), (g_any, g_out)]):
            half, columns = query_slice(peer)
            copies.append(
                to_peer(k, 1 + which, src.at[half, columns], dst.at[query_rows(c)], peer)
            )
            copies[-1].start()
    kv_out[key_rows(r, c), :] = packed[c // halves]
    half, columns = query_slice(c)
    fetches[2].wait()
    fetches[3].wait()
    own_query.wait()
    g_out[query_rows(c), :] = g_ref[half, columns]

    for h in range(KV_HEADS):
        cut = slice(h * LANES, (h + 1) * LANES)
        product = jnp.transpose(g_ref[:, cut].astype(f32) * o_ref[:, cut].astype(f32))
        sums = jnp.sum(product.reshape(MEMBERS, HEAD, rows), axis=1) * 0.125
        for u in range(rows // STRETCH):
            line = jnp.concatenate(
                [sums[m : m + 1, u * STRETCH : (u + 1) * STRETCH] for m in range(MEMBERS)], axis=1
            )
            each = part // STRETCH
            terms[h * halves + u // each, u % each : u % each + 1, :] = line
    for k in range(1, cols):
        peer = lax.rem(c + k, cols)
        copies.append(to_peer(k, 3, terms.at[peer], d_out.at[c], peer))
        copies[-1].start()
    d_out[c] = terms[c]

    def from_peer(k, which, dst):
        return remote(dst, dst, send_a.at[k, which], recv_a.at[k, which], (r, lax.rem(c + k, cols)))

    for k in range(1, cols):
        source = lax.rem(c + cols - k, cols)
        from_peer(k, 0, kv_out.at[key_rows(r, source)]).wait_recv()

    def whole(rank):
        return kv_out.at[pl.ds(pl.multiple_of(rank * block, block), block)]

    for k in range(1, ranks // 2):
        peer = lax.rem(r + 2 * k, ranks)
        copies.append(remote(whole(r), whole(r), send_z.at[k], recv_z.at[k], (peer, c)))
        copies[-1].start()
    copies.append(remote(whole(r), whole(r), send_s.at[0], recv_s.at[0], (sibling, c)))
    copies[-1].start()
    for k in range(1, ranks // 2):
        source = lax.rem(r + ranks - 2 * k, ranks)
        peer = lax.rem(r + 2 * k, ranks)
        here = whole(source)
        remote(here, here, send_z.at[k], recv_z.at[k], (peer, c)).wait_recv()
        copies.append(remote(here, here, send_s.at[k], recv_s.at[k], (sibling, c)))
        copies[-1].start()
    for k in range(ranks // 2):
        here = whole(lax.rem(sibling + ranks - 2 * k, ranks))
        remote(here, here, send_s.at[k], recv_s.at[k], (sibling, c)).wait_recv()
    for k in range(1, cols):
        source = lax.rem(c + cols - k, cols)
        from_peer(k, 1, q_out.at[query_rows(source)]).wait_recv()
        from_peer(k, 2, g_out.at[query_rows(source)]).wait_recv()
        from_peer(k, 3, d_out.at[source]).wait_recv()
    for copy in copies:
        copy.wait_send()


def gather(queries, out_grad, outputs, keys, values, ranks, cols):
    rows = queries.shape[0]
    part = rows // (cols // KV_HEADS)
    bf16 = jnp.bfloat16
    vmem = pl.BlockSpec(memory_space=pltpu.VMEM)
    dma = pltpu.SemaphoreType.DMA
    return pl.pallas_call(
        functools.partial(gather_kernel, ranks, cols),
        out_shape=(
            jax.ShapeDtypeStruct((cols * part, LANES), bf16),
            jax.ShapeDtypeStruct((cols * part, LANES), bf16),
            jax.ShapeDtypeStruct((cols, 8, LANES), jnp.float32),
            jax.ShapeDtypeStruct((ranks * cols * rows, 2 * HEAD), bf16),
        ),
        in_specs=[pl.BlockSpec(memory_space=pltpu.HBM)] * 5,
        out_specs=(vmem,) * 4,
        scratch_shapes=[
            pltpu.VMEM((KV_HEADS, rows, 2 * HEAD), bf16),
            pltpu.VMEM((cols, 8, LANES), jnp.float32),
            pltpu.VMEM((rows, HEADS * HEAD), bf16),
            pltpu.VMEM((rows, HEADS * HEAD), bf16),
            pltpu.VMEM((rows, KV_HEADS * HEAD), bf16),
            pltpu.VMEM((rows, KV_HEADS * HEAD), bf16),
            dma((5,)),
            dma((cols, 4)), dma((cols, 4)),
            dma((ranks // 2,)), dma((ranks // 2,)),
            dma((ranks // 2,)), dma((ranks // 2,)),
        ],
        compiler_params=pltpu.CompilerParams(
            collective_id=0, has_side_effects=True, vmem_limit_bytes=40 * 1024 * 1024
        ),
    )(queries, out_grad, outputs, keys, values)


def scatter_kernel(
    ranks, cols, dq_ref, dkv_ref, q_out, k_out, v_out,
    near, passing, far, share, last,
    send_q, recv_q, send_s, recv_s, send_z, recv_z, send_a, recv_a,
):
    f32, bf16 = jnp.float32, jnp.bfloat16
    r, c = lax.axis_index("qrow"), lax.axis_index("kcol")
    sibling = r + 1 - 2 * lax.rem(r, 2)
    rows = q_out.shape[0]
    halves = cols // KV_HEADS
    part = rows // halves
    block = cols * rows
    steps = ranks // 2
    greet(ranks, cols)

    def span(rank):
        return pl.ds(pl.multiple_of(rank * block, block), block)

    def query_rows(col):
        return pl.ds(pl.multiple_of(col * part, part), part)

    def query_slice(col):
        half = pl.ds(pl.multiple_of(lax.rem(col, halves) * part, part), part)
        return half, pl.ds(pl.multiple_of((col // halves) * LANES, LANES), LANES)

    copies = []
    order = list(range(1, steps)) + [0]
    for k in order:
        target = lax.rem(sibling + 2 * k, ranks)
        copies.append(
            remote(dkv_ref.at[span(target)], near.at[k], send_s.at[k], recv_s.at[k], (sibling, c))
        )
        copies[-1].start()
    for k in order:
        peer = lax.rem(r + 2 * k, ranks)
        remote(near.at[k], near.at[k], send_s.at[k], recv_s.at[k], (sibling, c)).wait_recv()
        both = dkv_ref[span(peer), :].astype(f32) + near[k].astype(f32)
        if k:
            passing[k] = both.astype(bf16)
            copies.append(
                remote(passing.at[k], far.at[k], send_z.at[k], recv_z.at[k], (peer, c))
            )
            copies[-1].start()
    half, columns = query_slice(c)
    for k in range(1, cols):
        peer = lax.rem(c + k, cols)
        copies.append(
            remote(
                dq_ref.at[query_rows(peer)], q_out.at[half, columns],
                send_q.at[k], recv_q.at[k], (r, peer),
            )
        )
        copies[-1].start()
    q_out[half, columns] = dq_ref[query_rows(c), :]
    total = both
    for k in range(1, steps):
        peer = lax.rem(r + 2 * k, ranks)
        remote(far.at[k], far.at[k], send_z.at[k], recv_z.at[k], (peer, c)).wait_recv()
        total = total + far[k].astype(f32)
    share[...] = total.astype(bf16)

    def share_rows(col):
        return pl.ds(pl.multiple_of(col * rows, rows), rows)

    for k in range(1, cols):
        peer = lax.rem(c + k, cols)
        copies.append(
            remote(share.at[share_rows(peer)], last.at[c], send_a.at[k], recv_a.at[k], (r, peer))
        )
        copies[-1].start()
    last[c] = share[share_rows(c), :]
    for k in range(1, cols):
        peer = lax.rem(c + k, cols)
        here = last.at[lax.rem(c + cols - k, cols)]
        remote(here, here, send_a.at[k], recv_a.at[k], (r, peer)).wait_recv()
    k_parts, v_parts = [], []
    for h in range(KV_HEADS):
        whole = last[h * halves].astype(f32)
        for other in range(1, halves):
            whole = whole + last[h * halves + other].astype(f32)
        v_parts.append(whole[:, :HEAD])
        k_parts.append(whole[:, HEAD:])
    k_out[...] = jnp.concatenate(k_parts, axis=1).astype(bf16)
    v_out[...] = jnp.concatenate(v_parts, axis=1).astype(bf16)
    for k in range(1, cols):
        peer = lax.rem(c + k, cols)
        half, columns = query_slice(lax.rem(c + cols - k, cols))
        here = q_out.at[half, columns]
        remote(dq_ref.at[query_rows(peer)], here, send_q.at[k], recv_q.at[k], (r, peer)).wait_recv()
    for copy in copies:
        copy.wait_send()


def scatter(dq, dkv, rows, ranks, cols):
    bf16 = jnp.bfloat16
    vmem = pl.BlockSpec(memory_space=pltpu.VMEM)
    dma = pltpu.SemaphoreType.DMA
    block = cols * rows
    return pl.pallas_call(
        functools.partial(scatter_kernel, ranks, cols),
        out_shape=(
            jax.ShapeDtypeStruct((rows, HEADS * HEAD), bf16),
            jax.ShapeDtypeStruct((rows, KV_HEADS * HEAD), bf16),
            jax.ShapeDtypeStruct((rows, KV_HEADS * HEAD), bf16),
        ),
        in_specs=[vmem] * 2,
        out_specs=(vmem,) * 3,
        scratch_shapes=[
            pltpu.VMEM((ranks // 2, block, 2 * HEAD), bf16),
            pltpu.VMEM((ranks // 2, block, 2 * HEAD), bf16),
            pltpu.VMEM((ranks // 2, block, 2 * HEAD), bf16),
            pltpu.VMEM((block, 2 * HEAD), bf16),
            pltpu.VMEM((cols, rows, 2 * HEAD), bf16),
            dma((cols,)), dma((cols,)),
            dma((ranks // 2,)), dma((ranks // 2,)),
            dma((ranks // 2,)), dma((ranks // 2,)),
            dma((cols,)), dma((cols,)),
        ],
        compiler_params=pltpu.CompilerParams(
            collective_id=1, has_side_effects=True, vmem_limit_bytes=40 * 1024 * 1024
        ),
    )(dq, dkv)


def per_device(queries, keys, values, outputs, out_grad, positions):
    rows = queries.shape[0]
    ranks = lax.axis_size("qrow")
    cols = lax.axis_size("kcol")
    q, g, d, kv = gather(queries, out_grad, outputs, keys, values, ranks, cols)
    dq, dkv = attention(positions, q, g, d, kv, ranks, cols)
    return scatter(dq, dkv, rows, ranks, cols)


def solution(mesh):
    in_specs = (
        P(("kcol", "qrow"), None),
        P(("qrow", "kcol"), None),
        P(("qrow", "kcol"), None),
        P(("kcol", "qrow"), None),
        P(("kcol", "qrow"), None),
        P(),
    )
    out_specs = (P(("kcol", "qrow"), None), P(("qrow", "kcol"), None), P(("qrow", "kcol"), None))
    return jax.shard_map(
        per_device, mesh=mesh, in_specs=in_specs, out_specs=out_specs, check_vma=False
    )
```

```python
import functools

import jax
import jax.numpy as jnp
from jax import lax
from jax.experimental import pallas as pl
from jax.experimental.pallas import tpu as pltpu
from jax.sharding import PartitionSpec as P

HEADS = 16
KV_HEADS = 4
HEAD = 64
STRETCH = 64
MEMBERS = HEADS // KV_HEADS
LANES = MEMBERS * STRETCH
KB = 1024
CUT = 256
GRANT = 60 << 20


def attention_kernel(
    ranks, cols, positions, q_ref, g_ref, d_ref, kv_ref, dq_ref, dkv_ref,
    kvs, kts, scr, acc, xq_t, xg_t, xx,
):
    tokens = kv_ref.shape[0]
    stretches = tokens // STRETCH
    f32, bf16 = jnp.float32, jnp.bfloat16
    rows = tokens // (ranks * cols)
    halves = cols // KV_HEADS
    part = rows // halves
    each = part // STRETCH
    rank = lax.axis_index("qrow")
    half = lax.rem(lax.axis_index("kcol"), halves)
    lane = lax.broadcasted_iota(jnp.int32, (1, 2 * HEAD), 1)

    def place(t, c):
        src = pl.multiple_of(t * STRETCH, STRETCH)
        dst = pl.multiple_of(positions[src], STRETCH)
        kvs[pl.ds(dst, STRETCH), :] = kv_ref[pl.ds(src, STRETCH), :]
        return c

    lax.fori_loop(0, stretches, place, 0, unroll=8)

    def turn(j, c):
        at = pl.multiple_of(j * KB, KB)
        kts[j] = jnp.transpose(kvs[pl.ds(at, KB), :])[HEAD:, :]
        acc[pl.ds(at, KB), :] = jnp.zeros((KB, 2 * HEAD), f32)
        return c

    lax.fori_loop(0, tokens // KB, turn, 0)

    def head_rows(block, upper):
        pieces = []
        for h in range(MEMBERS):
            pair = block[:, (h // 2) * 2 * HEAD : (h // 2 + 1) * 2 * HEAD]
            if (h % 2 == 1) != upper:
                pair = pltpu.roll(pair, HEAD, 1)
            pieces.append(jnp.where((lane >= HEAD) == upper, pair, 0.0))
        return jnp.concatenate(pieces, axis=0)

    def one_stretch(st, c):
        at = pl.multiple_of(st * STRETCH, STRETCH)
        origin = ((st // each) * ranks + rank) * rows + half * part + lax.rem(st, each) * STRETCH
        start = positions[origin]
        g_rows = head_rows(g_ref[pl.ds(at, STRETCH), :].astype(f32), False)
        q_rows = head_rows(q_ref[pl.ds(at, STRETCH), :].astype(f32) * 0.125, True)
        delta = d_ref[st // each, pl.ds(lax.rem(st, each), 1), :]
        xx[:LANES] = g_rows.astype(bf16)
        xx[LANES:] = q_rows.astype(bf16)
        turned = jnp.transpose(g_rows + q_rows).astype(bf16)
        none = jnp.zeros((HEAD, LANES), bf16)
        xg_t[:HEAD] = turned[:HEAD]
        xg_t[HEAD:] = none
        xq_t[:HEAD] = none
        xq_t[HEAD:] = turned[HEAD:]
        full = start // KB

        kr = pl.multiple_of(full * KB, KB)
        quarter = (start - kr) // CUT

        def at_edge(step, carry):
            sizes = range(CUT, KB + 1, CUT)
            return lax.switch(quarter, [functools.partial(step, full, size=n) for n in sizes], carry)

        def fold(s, size):
            return s.reshape(size // 8, 8, LANES)

        def keys_of(j, size):
            return pl.ds(pl.multiple_of(j * KB, KB), size)

        def first(j, m, size=KB, edge=False):
            s = jnp.dot(kvs[keys_of(j, size), :], xq_t[...], preferred_element_type=f32)
            if edge:
                key_pos = kr - start + lax.broadcasted_iota(jnp.int32, (size, LANES), 0)
                row_pos = lax.rem(lax.broadcasted_iota(jnp.int32, (1, LANES), 1), STRETCH)
                s = jnp.where(key_pos <= row_pos, s, -1e30)
            scr[keys_of(j, size), :] = s
            return jnp.maximum(m, jnp.max(fold(s, size), axis=0))

        m = lax.fori_loop(0, full, first, jnp.full((8, LANES), -1e30, f32))
        m = at_edge(functools.partial(first, edge=True), m)
        m = jnp.max(m, axis=0, keepdims=True)

        def second(j, total, size=KB):
            e = jnp.exp(scr[keys_of(j, size), :] - m)
            scr[keys_of(j, size), :] = e
            return total + jnp.sum(fold(e, size), axis=0)

        total = lax.fori_loop(0, full, second, jnp.zeros((8, LANES), f32))
        total = at_edge(second, total)
        inverse = 1.0 / jnp.sum(total, axis=0, keepdims=True)

        def third(j, dq, size=KB):
            w = scr[keys_of(j, size), :] * inverse
            dw = jnp.dot(kvs[keys_of(j, size), :], xg_t[...], preferred_element_type=f32)
            ds = (w * (dw - delta)).astype(bf16)
            both = jnp.concatenate([w.astype(bf16), ds], axis=1)
            acc[keys_of(j, size), :] += jnp.dot(both, xx[...], preferred_element_type=f32)
            return dq + jnp.dot(kts[j, :, :size], ds, preferred_element_type=f32)

        dq = lax.fori_loop(0, full, third, jnp.zeros((HEAD, LANES), f32))
        dq = at_edge(third, dq)
        flat = jnp.concatenate([dq[:, h * STRETCH : (h + 1) * STRETCH] for h in range(MEMBERS)], axis=0)
        dq_ref[pl.ds(at, STRETCH), :] = jnp.transpose(flat).astype(bf16)
        return c

    lax.fori_loop(0, q_ref.shape[0] // STRETCH, one_stretch, 0)
    gain = jnp.where(lane < HEAD, 1.0, 8.0).astype(f32)

    def restore(t, c):
        dst = pl.multiple_of(t * STRETCH, STRETCH)
        src = pl.multiple_of(positions[dst], STRETCH)
        dkv_ref[pl.ds(dst, STRETCH), :] = (acc[pl.ds(src, STRETCH), :] * gain).astype(dkv_ref.dtype)
        return c

    lax.fori_loop(0, stretches, restore, 0, unroll=8)


def attention(positions, q, g, d, kv, ranks, cols):
    tokens = kv.shape[0]
    vmem = pl.BlockSpec(memory_space=pltpu.VMEM)
    smem = pl.BlockSpec(memory_space=pltpu.SMEM)
    bf16, f32 = jnp.bfloat16, jnp.float32
    return pl.pallas_call(
        functools.partial(attention_kernel, ranks, cols),
        out_shape=(
            jax.ShapeDtypeStruct(q.shape, bf16),
            jax.ShapeDtypeStruct((tokens, 2 * HEAD), bf16),
        ),
        in_specs=[smem, vmem, vmem, vmem, vmem],
        out_specs=(vmem, vmem),
        scratch_shapes=[
            pltpu.VMEM((tokens, 2 * HEAD), bf16),
            pltpu.VMEM((tokens // KB, HEAD, KB), bf16),
            pltpu.VMEM((tokens, LANES), f32),
            pltpu.VMEM((tokens, 2 * HEAD), f32),
            pltpu.VMEM((2 * HEAD, LANES), bf16),
            pltpu.VMEM((2 * HEAD, LANES), bf16),
            pltpu.VMEM((2 * LANES, 2 * HEAD), bf16),
        ],
        compiler_params=pltpu.CompilerParams(vmem_limit_bytes=(8 << 20) + tokens * 2560),
    )(positions, q, g, d, kv)


def greet(ranks, cols):
    r, c = lax.axis_index("qrow"), lax.axis_index("kcol")
    barrier = pltpu.get_barrier_semaphore()
    count = 0
    for k in range(1, cols):
        signal(barrier, (r, lax.rem(c + k, cols)))
        count += 1
    for k in range(1, ranks // 2):
        signal(barrier, (lax.rem(r + 2 * k, ranks), c))
        count += 1
    signal(barrier, (r + 1 - 2 * lax.rem(r, 2), c))
    pl.semaphore_wait(barrier, count + 1)


def signal(semaphore, device):
    pl.semaphore_signal(
        semaphore, inc=1, device_id=device, device_id_type=pl.DeviceIdType.MESH
    )


def remote(src, dst, send, recv, device):
    return pltpu.make_async_remote_copy(
        src_ref=src, dst_ref=dst, send_sem=send, recv_sem=recv,
        device_id=device, device_id_type=pl.DeviceIdType.MESH,
    )


def gather_kernel(
    ranks, cols, q_any, g_any, o_any, k_any, v_any, q_out, g_out, d_out, kv_out,
    packed, terms, g_ref, o_ref, k_ref, v_ref, fetched, send_a, recv_a, send_z, recv_z, send_s, recv_s,
):
    f32, bf16 = jnp.float32, jnp.bfloat16
    r, c = lax.axis_index("qrow"), lax.axis_index("kcol")
    sibling = r + 1 - 2 * lax.rem(r, 2)
    rows = q_any.shape[0]
    halves = cols // KV_HEADS
    part = rows // halves
    block = cols * rows
    pairs = [(k_any, k_ref), (v_any, v_ref), (g_any, g_ref), (o_any, o_ref)]
    fetches = [pltpu.make_async_copy(a, b, fetched.at[n]) for n, (a, b) in enumerate(pairs)]
    for fetch in fetches:
        fetch.start()

    def key_rows(rank, col):
        return pl.ds(pl.multiple_of((rank * cols + col) * rows, rows), rows)

    def query_rows(col):
        return pl.ds(pl.multiple_of(col * part, part), part)

    def query_slice(col):
        half = pl.ds(pl.multiple_of(lax.rem(col, halves) * part, part), part)
        return half, pl.ds(pl.multiple_of((col // halves) * LANES, LANES), LANES)

    half, columns = query_slice(c)
    own_query = pltpu.make_async_copy(
        q_any.at[half, columns], q_out.at[query_rows(c)], fetched.at[4]
    )
    own_query.start()
    fetches[0].wait()
    fetches[1].wait()
    for h in range(KV_HEADS):
        cut = slice(h * HEAD, (h + 1) * HEAD)
        packed[h] = jnp.concatenate(
            [(v_ref[:, cut].astype(f32) * 0.125).astype(bf16), k_ref[:, cut]], axis=1
        )

    greet(ranks, cols)

    def to_peer(k, which, src, dst, peer):
        return remote(src, dst, send_a.at[k, which], recv_a.at[k, which], (r, peer))

    copies = []
    for k in range(1, cols):
        peer = lax.rem(c + k, cols)
        copies.append(
            to_peer(k, 0, packed.at[peer // halves], kv_out.at[key_rows(r, c)], peer)
        )
        copies[-1].start()
    for k in range(1, cols):
        peer = lax.rem(c + k, cols)
        for which, (src, dst) in enumerate([(q_any, q_out), (g_any, g_out)]):
            half, columns = query_slice(peer)
            copies.append(
                to_peer(k, 1 + which, src.at[half, columns], dst.at[query_rows(c)], peer)
            )
            copies[-1].start()
    kv_out[key_rows(r, c), :] = packed[c // halves]
    half, columns = query_slice(c)
    fetches[2].wait()
    fetches[3].wait()
    own_query.wait()
    g_out[query_rows(c), :] = g_ref[half, columns]

    for h in range(KV_HEADS):
        cut = slice(h * LANES, (h + 1) * LANES)
        product = jnp.transpose(g_ref[:, cut].astype(f32) * o_ref[:, cut].astype(f32))
        sums = jnp.sum(product.reshape(MEMBERS, HEAD, rows), axis=1) * 0.125
        for u in range(rows // STRETCH):
            line = jnp.concatenate(
                [sums[m : m + 1, u * STRETCH : (u + 1) * STRETCH] for m in range(MEMBERS)], axis=1
            )
            each = part // STRETCH
            terms[h * halves + u // each, u % each : u % each + 1, :] = line
    for k in range(1, cols):
        peer = lax.rem(c + k, cols)
        copies.append(to_peer(k, 3, terms.at[peer], d_out.at[c], peer))
        copies[-1].start()
    d_out[c] = terms[c]

    def from_peer(k, which, dst):
        return remote(dst, dst, send_a.at[k, which], recv_a.at[k, which], (r, lax.rem(c + k, cols)))

    for k in range(1, cols):
        source = lax.rem(c + cols - k, cols)
        from_peer(k, 0, kv_out.at[key_rows(r, source)]).wait_recv()

    def whole(rank):
        return kv_out.at[pl.ds(pl.multiple_of(rank * block, block), block)]

    for k in range(1, ranks // 2):
        peer = lax.rem(r + 2 * k, ranks)
        copies.append(remote(whole(r), whole(r), send_z.at[k], recv_z.at[k], (peer, c)))
        copies[-1].start()
    copies.append(remote(whole(r), whole(r), send_s.at[0], recv_s.at[0], (sibling, c)))
    copies[-1].start()
    for k in range(1, ranks // 2):
        source = lax.rem(r + ranks - 2 * k, ranks)
        peer = lax.rem(r + 2 * k, ranks)
        here = whole(source)
        remote(here, here, send_z.at[k], recv_z.at[k], (peer, c)).wait_recv()
        copies.append(remote(here, here, send_s.at[k], recv_s.at[k], (sibling, c)))
        copies[-1].start()
    for k in range(ranks // 2):
        here = whole(lax.rem(sibling + ranks - 2 * k, ranks))
        remote(here, here, send_s.at[k], recv_s.at[k], (sibling, c)).wait_recv()
    for k in range(1, cols):
        source = lax.rem(c + cols - k, cols)
        from_peer(k, 1, q_out.at[query_rows(source)]).wait_recv()
        from_peer(k, 2, g_out.at[query_rows(source)]).wait_recv()
        from_peer(k, 3, d_out.at[source]).wait_recv()
    for copy in copies:
        copy.wait_send()


def gather(queries, out_grad, outputs, keys, values, ranks, cols):
    rows = queries.shape[0]
    part = rows // (cols // KV_HEADS)
    bf16 = jnp.bfloat16
    vmem = pl.BlockSpec(memory_space=pltpu.VMEM)
    dma = pltpu.SemaphoreType.DMA
    return pl.pallas_call(
        functools.partial(gather_kernel, ranks, cols),
        out_shape=(
            jax.ShapeDtypeStruct((cols * part, LANES), bf16),
            jax.ShapeDtypeStruct((cols * part, LANES), bf16),
            jax.ShapeDtypeStruct((cols, 8, LANES), jnp.float32),
            jax.ShapeDtypeStruct((ranks * cols * rows, 2 * HEAD), bf16),
        ),
        in_specs=[pl.BlockSpec(memory_space=pltpu.HBM)] * 5,
        out_specs=(vmem,) * 4,
        scratch_shapes=[
            pltpu.VMEM((KV_HEADS, rows, 2 * HEAD), bf16),
            pltpu.VMEM((cols, 8, LANES), jnp.float32),
            pltpu.VMEM((rows, HEADS * HEAD), bf16),
            pltpu.VMEM((rows, HEADS * HEAD), bf16),
            pltpu.VMEM((rows, KV_HEADS * HEAD), bf16),
            pltpu.VMEM((rows, KV_HEADS * HEAD), bf16),
            dma((5,)),
            dma((cols, 4)), dma((cols, 4)),
            dma((ranks // 2,)), dma((ranks // 2,)),
            dma((ranks // 2,)), dma((ranks // 2,)),
        ],
        compiler_params=pltpu.CompilerParams(
            collective_id=0, has_side_effects=True, vmem_limit_bytes=GRANT
        ),
    )(queries, out_grad, outputs, keys, values)


def scatter_kernel(
    ranks, cols, dq_ref, dkv_ref, q_out, k_out, v_out,
    near, passing, far, share, last,
    send_q, recv_q, send_s, recv_s, send_z, recv_z, send_a, recv_a,
):
    f32, bf16 = jnp.float32, jnp.bfloat16
    r, c = lax.axis_index("qrow"), lax.axis_index("kcol")
    sibling = r + 1 - 2 * lax.rem(r, 2)
    rows = q_out.shape[0]
    halves = cols // KV_HEADS
    part = rows // halves
    block = cols * rows
    steps = ranks // 2
    greet(ranks, cols)

    def span(rank):
        return pl.ds(pl.multiple_of(rank * block, block), block)

    def query_rows(col):
        return pl.ds(pl.multiple_of(col * part, part), part)

    def query_slice(col):
        half = pl.ds(pl.multiple_of(lax.rem(col, halves) * part, part), part)
        return half, pl.ds(pl.multiple_of((col // halves) * LANES, LANES), LANES)

    copies = []
    order = list(range(1, steps)) + [0]
    for k in order:
        target = lax.rem(sibling + 2 * k, ranks)
        copies.append(
            remote(dkv_ref.at[span(target)], near.at[k], send_s.at[k], recv_s.at[k], (sibling, c))
        )
        copies[-1].start()
    for k in order:
        peer = lax.rem(r + 2 * k, ranks)
        remote(near.at[k], near.at[k], send_s.at[k], recv_s.at[k], (sibling, c)).wait_recv()
        both = dkv_ref[span(peer), :].astype(f32) + near[k].astype(f32)
        if k:
            passing[k] = both.astype(bf16)
            copies.append(
                remote(passing.at[k], far.at[k], send_z.at[k], recv_z.at[k], (peer, c))
            )
            copies[-1].start()
    half, columns = query_slice(c)
    for k in range(1, cols):
        peer = lax.rem(c + k, cols)
        copies.append(
            remote(
                dq_ref.at[query_rows(peer)], q_out.at[half, columns],
                send_q.at[k], recv_q.at[k], (r, peer),
            )
        )
        copies[-1].start()
    q_out[half, columns] = dq_ref[query_rows(c), :]
    total = both
    for k in range(1, steps):
        peer = lax.rem(r + 2 * k, ranks)
        remote(far.at[k], far.at[k], send_z.at[k], recv_z.at[k], (peer, c)).wait_recv()
        total = total + far[k].astype(f32)
    share[...] = total.astype(bf16)

    def share_rows(col):
        return pl.ds(pl.multiple_of(col * rows, rows), rows)

    for k in range(1, cols):
        peer = lax.rem(c + k, cols)
        copies.append(
            remote(share.at[share_rows(peer)], last.at[c], send_a.at[k], recv_a.at[k], (r, peer))
        )
        copies[-1].start()
    last[c] = share[share_rows(c), :]
    for k in range(1, cols):
        peer = lax.rem(c + k, cols)
        here = last.at[lax.rem(c + cols - k, cols)]
        remote(here, here, send_a.at[k], recv_a.at[k], (r, peer)).wait_recv()
    k_parts, v_parts = [], []
    for h in range(KV_HEADS):
        whole = last[h * halves].astype(f32)
        for other in range(1, halves):
            whole = whole + last[h * halves + other].astype(f32)
        v_parts.append(whole[:, :HEAD])
        k_parts.append(whole[:, HEAD:])
    k_out[...] = jnp.concatenate(k_parts, axis=1).astype(bf16)
    v_out[...] = jnp.concatenate(v_parts, axis=1).astype(bf16)
    for k in range(1, cols):
        peer = lax.rem(c + k, cols)
        half, columns = query_slice(lax.rem(c + cols - k, cols))
        here = q_out.at[half, columns]
        remote(dq_ref.at[query_rows(peer)], here, send_q.at[k], recv_q.at[k], (r, peer)).wait_recv()
    for copy in copies:
        copy.wait_send()


def scatter(dq, dkv, rows, ranks, cols):
    bf16 = jnp.bfloat16
    vmem = pl.BlockSpec(memory_space=pltpu.VMEM)
    dma = pltpu.SemaphoreType.DMA
    block = cols * rows
    return pl.pallas_call(
        functools.partial(scatter_kernel, ranks, cols),
        out_shape=(
            jax.ShapeDtypeStruct((rows, HEADS * HEAD), bf16),
            jax.ShapeDtypeStruct((rows, KV_HEADS * HEAD), bf16),
            jax.ShapeDtypeStruct((rows, KV_HEADS * HEAD), bf16),
        ),
        in_specs=[vmem] * 2,
        out_specs=(vmem,) * 3,
        scratch_shapes=[
            pltpu.VMEM((ranks // 2, block, 2 * HEAD), bf16),
            pltpu.VMEM((ranks // 2, block, 2 * HEAD), bf16),
            pltpu.VMEM((ranks // 2, block, 2 * HEAD), bf16),
            pltpu.VMEM((block, 2 * HEAD), bf16),
            pltpu.VMEM((cols, rows, 2 * HEAD), bf16),
            dma((cols,)), dma((cols,)),
            dma((ranks // 2,)), dma((ranks // 2,)),
            dma((ranks // 2,)), dma((ranks // 2,)),
            dma((cols,)), dma((cols,)),
        ],
        compiler_params=pltpu.CompilerParams(
            collective_id=1, has_side_effects=True, vmem_limit_bytes=40 * 1024 * 1024
        ),
    )(dq, dkv)


def per_device(queries, keys, values, outputs, out_grad, positions):
    rows = queries.shape[0]
    ranks = lax.axis_size("qrow")
    cols = lax.axis_size("kcol")
    q, g, d, kv = gather(queries, out_grad, outputs, keys, values, ranks, cols)
    dq, dkv = attention(positions, q, g, d, kv, ranks, cols)
    return scatter(dq, dkv, rows, ranks, cols)


def solution(mesh):
    in_specs = (
        P(("kcol", "qrow"), None),
        P(("qrow", "kcol"), None),
        P(("qrow", "kcol"), None),
        P(("kcol", "qrow"), None),
        P(("kcol", "qrow"), None),
        P(),
    )
    out_specs = (P(("kcol", "qrow"), None), P(("qrow", "kcol"), None), P(("qrow", "kcol"), None))
    return jax.shard_map(
        per_device, mesh=mesh, in_specs=in_specs, out_specs=out_specs, check_vma=False
    )
```

```python
import functools

import jax
import jax.numpy as jnp
from jax import lax
from jax.experimental import pallas as pl
from jax.experimental.pallas import tpu as pltpu
from jax.sharding import PartitionSpec as P

HEADS = 16
KV_HEADS = 4
HEAD = 64
STRETCH = 64
MEMBERS = HEADS // KV_HEADS
LANES = MEMBERS * STRETCH
KB = 1024
CUT = 256
GRANT = 60 << 20


def attention_kernel(
    ranks, cols, positions, q_ref, g_ref, d_ref, kv_ref, dq_ref, dkv_ref,
    kvs, kts, scr, acc, xq_t, xg_t, xx,
):
    tokens = kv_ref.shape[0]
    stretches = tokens // STRETCH
    f32, bf16 = jnp.float32, jnp.bfloat16
    rows = tokens // (ranks * cols)
    halves = cols // KV_HEADS
    part = rows // halves
    each = part // STRETCH
    rank = lax.axis_index("qrow")
    half = lax.rem(lax.axis_index("kcol"), halves)
    lane = lax.broadcasted_iota(jnp.int32, (1, 2 * HEAD), 1)

    def place(t, c):
        src = pl.multiple_of(t * STRETCH, STRETCH)
        dst = pl.multiple_of(positions[src], STRETCH)
        kvs[pl.ds(dst, STRETCH), :] = kv_ref[pl.ds(src, STRETCH), :]
        return c

    lax.fori_loop(0, stretches, place, 0, unroll=8)

    def turn(j, c):
        at = pl.multiple_of(j * KB, KB)
        kts[j] = jnp.transpose(kvs[pl.ds(at, KB), :])[HEAD:, :]
        acc[pl.ds(at, KB), :] = jnp.zeros((KB, 2 * HEAD), f32)
        return c

    lax.fori_loop(0, tokens // KB, turn, 0)

    def head_rows(block, upper):
        pieces = []
        for h in range(MEMBERS):
            pair = block[:, (h // 2) * 2 * HEAD : (h // 2 + 1) * 2 * HEAD]
            if (h % 2 == 1) != upper:
                pair = pltpu.roll(pair, HEAD, 1)
            pieces.append(jnp.where((lane >= HEAD) == upper, pair, 0.0))
        return jnp.concatenate(pieces, axis=0)

    def one_stretch(st, c):
        at = pl.multiple_of(st * STRETCH, STRETCH)
        origin = ((st // each) * ranks + rank) * rows + half * part + lax.rem(st, each) * STRETCH
        start = positions[origin]
        g_rows = head_rows(g_ref[pl.ds(at, STRETCH), :].astype(f32), False)
        q_rows = head_rows(q_ref[pl.ds(at, STRETCH), :].astype(f32) * 0.125, True)
        delta = d_ref[st // each, pl.ds(lax.rem(st, each), 1), :]
        xx[:LANES] = g_rows.astype(bf16)
        xx[LANES:] = q_rows.astype(bf16)
        turned = jnp.transpose(g_rows + q_rows).astype(bf16)
        none = jnp.zeros((HEAD, LANES), bf16)
        xg_t[:HEAD] = turned[:HEAD]
        xg_t[HEAD:] = none
        xq_t[:HEAD] = none
        xq_t[HEAD:] = turned[HEAD:]
        full = start // KB

        kr = pl.multiple_of(full * KB, KB)
        quarter = (start - kr) // CUT

        def at_edge(step, carry):
            sizes = range(CUT, KB + 1, CUT)
            return lax.switch(quarter, [functools.partial(step, full, size=n) for n in sizes], carry)

        def fold(s, size):
            return s.reshape(size // 8, 8, LANES)

        def keys_of(j, size):
            return pl.ds(pl.multiple_of(j * KB, KB), size)

        def first(j, m, size=KB, edge=False):
            s = jnp.dot(kvs[keys_of(j, size), :], xq_t[...], preferred_element_type=f32)
            if edge:
                key_pos = kr - start + lax.broadcasted_iota(jnp.int32, (size, LANES), 0)
                row_pos = lax.rem(lax.broadcasted_iota(jnp.int32, (1, LANES), 1), STRETCH)
                s = jnp.where(key_pos <= row_pos, s, -1e30)
            scr[keys_of(j, size), :] = s
            return jnp.maximum(m, jnp.max(fold(s, size), axis=0))

        m = lax.fori_loop(0, full, first, jnp.full((8, LANES), -1e30, f32))
        m = at_edge(functools.partial(first, edge=True), m)
        m = jnp.max(m, axis=0, keepdims=True)

        def second(j, total, size=KB):
            e = jnp.exp(scr[keys_of(j, size), :] - m)
            scr[keys_of(j, size), :] = e
            return total + jnp.sum(fold(e, size), axis=0)

        total = lax.fori_loop(0, full, second, jnp.zeros((8, LANES), f32))
        total = at_edge(second, total)
        inverse = 1.0 / jnp.sum(total, axis=0, keepdims=True)

        def third(j, dq, size=KB):
            w = scr[keys_of(j, size), :] * inverse
            dw = jnp.dot(kvs[keys_of(j, size), :], xg_t[...], preferred_element_type=f32)
            ds = (w * (dw - delta)).astype(bf16)
            both = jnp.concatenate([w.astype(bf16), ds], axis=1)
            acc[keys_of(j, size), :] += jnp.dot(both, xx[...], preferred_element_type=f32)
            return dq + jnp.dot(kts[j, :, :size], ds, preferred_element_type=f32)

        dq = lax.fori_loop(0, full, third, jnp.zeros((HEAD, LANES), f32))
        dq = at_edge(third, dq)
        flat = jnp.concatenate([dq[:, h * STRETCH : (h + 1) * STRETCH] for h in range(MEMBERS)], axis=0)
        dq_ref[pl.ds(at, STRETCH), :] = jnp.transpose(flat).astype(bf16)
        return c

    lax.fori_loop(0, q_ref.shape[0] // STRETCH, one_stretch, 0)
    gain = jnp.where(lane < HEAD, 1.0, 8.0).astype(f32)

    def restore(t, c):
        dst = pl.multiple_of(t * STRETCH, STRETCH)
        src = pl.multiple_of(positions[dst], STRETCH)
        dkv_ref[pl.ds(dst, STRETCH), :] = (acc[pl.ds(src, STRETCH), :] * gain).astype(dkv_ref.dtype)
        return c

    lax.fori_loop(0, stretches, restore, 0, unroll=8)


def attention(positions, q, g, d, kv, ranks, cols):
    tokens = kv.shape[0]
    vmem = pl.BlockSpec(memory_space=pltpu.VMEM)
    smem = pl.BlockSpec(memory_space=pltpu.SMEM)
    bf16, f32 = jnp.bfloat16, jnp.float32
    return pl.pallas_call(
        functools.partial(attention_kernel, ranks, cols),
        out_shape=(
            jax.ShapeDtypeStruct(q.shape, bf16),
            jax.ShapeDtypeStruct((tokens, 2 * HEAD), bf16),
        ),
        in_specs=[smem, vmem, vmem, vmem, vmem],
        out_specs=(vmem, vmem),
        scratch_shapes=[
            pltpu.VMEM((tokens, 2 * HEAD), bf16),
            pltpu.VMEM((tokens // KB, HEAD, KB), bf16),
            pltpu.VMEM((tokens, LANES), f32),
            pltpu.VMEM((tokens, 2 * HEAD), f32),
            pltpu.VMEM((2 * HEAD, LANES), bf16),
            pltpu.VMEM((2 * HEAD, LANES), bf16),
            pltpu.VMEM((2 * LANES, 2 * HEAD), bf16),
        ],
        compiler_params=pltpu.CompilerParams(vmem_limit_bytes=(8 << 20) + tokens * 2560),
    )(positions, q, g, d, kv)


def greet(ranks, cols):
    r, c = lax.axis_index("qrow"), lax.axis_index("kcol")
    barrier = pltpu.get_barrier_semaphore()
    count = 0
    for k in range(1, cols):
        signal(barrier, (r, lax.rem(c + k, cols)))
        count += 1
    for k in range(1, ranks // 2):
        signal(barrier, (lax.rem(r + 2 * k, ranks), c))
        count += 1
    signal(barrier, (r + 1 - 2 * lax.rem(r, 2), c))
    pl.semaphore_wait(barrier, count + 1)


def signal(semaphore, device):
    pl.semaphore_signal(
        semaphore, inc=1, device_id=device, device_id_type=pl.DeviceIdType.MESH
    )


def remote(src, dst, send, recv, device):
    return pltpu.make_async_remote_copy(
        src_ref=src, dst_ref=dst, send_sem=send, recv_sem=recv,
        device_id=device, device_id_type=pl.DeviceIdType.MESH,
    )


def gather_kernel(
    ranks, cols, q_any, g_any, o_any, k_any, v_any, q_out, g_out, d_out, kv_out,
    packed, terms, g_ref, o_ref, k_ref, v_ref, fetched, send_a, recv_a, send_z, recv_z, send_s, recv_s,
):
    f32, bf16 = jnp.float32, jnp.bfloat16
    r, c = lax.axis_index("qrow"), lax.axis_index("kcol")
    sibling = r + 1 - 2 * lax.rem(r, 2)
    rows = q_any.shape[0]
    halves = cols // KV_HEADS
    part = rows // halves
    block = cols * rows
    pairs = [(k_any, k_ref), (v_any, v_ref), (g_any, g_ref), (o_any, o_ref)]
    fetches = [pltpu.make_async_copy(a, b, fetched.at[n]) for n, (a, b) in enumerate(pairs)]
    for fetch in fetches:
        fetch.start()

    def key_rows(rank, col):
        return pl.ds(pl.multiple_of((rank * cols + col) * rows, rows), rows)

    def query_rows(col):
        return pl.ds(pl.multiple_of(col * part, part), part)

    def query_slice(col):
        half = pl.ds(pl.multiple_of(lax.rem(col, halves) * part, part), part)
        return half, pl.ds(pl.multiple_of((col // halves) * LANES, LANES), LANES)

    half, columns = query_slice(c)
    own_query = pltpu.make_async_copy(
        q_any.at[half, columns], q_out.at[query_rows(c)], fetched.at[4]
    )
    own_query.start()
    fetches[0].wait()
    fetches[1].wait()
    for h in range(KV_HEADS):
        cut = slice(h * HEAD, (h + 1) * HEAD)
        packed[h] = jnp.concatenate(
            [(v_ref[:, cut].astype(f32) * 0.125).astype(bf16), k_ref[:, cut]], axis=1
        )

    greet(ranks, cols)

    def to_peer(k, which, src, dst, peer):
        return remote(src, dst, send_a.at[k, which], recv_a.at[k, which], (r, peer))

    copies = []
    for k in range(1, cols):
        peer = lax.rem(c + k, cols)
        copies.append(
            to_peer(k, 0, packed.at[peer // halves], kv_out.at[key_rows(r, c)], peer)
        )
        copies[-1].start()
    for k in range(1, cols):
        peer = lax.rem(c + k, cols)
        for which, (src, dst) in enumerate([(q_any, q_out), (g_any, g_out)]):
            half, columns = query_slice(peer)
            copies.append(
                to_peer(k, 1 + which, src.at[half, columns], dst.at[query_rows(c)], peer)
            )
            copies[-1].start()
    kv_out[key_rows(r, c), :] = packed[c // halves]
    def from_peer(k, which, dst):
        return remote(dst, dst, send_a.at[k, which], recv_a.at[k, which], (r, lax.rem(c + k, cols)))

    for k in range(1, cols):
        source = lax.rem(c + cols - k, cols)
        from_peer(k, 0, kv_out.at[key_rows(r, source)]).wait_recv()

    def whole(rank):
        return kv_out.at[pl.ds(pl.multiple_of(rank * block, block), block)]

    for k in range(1, ranks // 2):
        peer = lax.rem(r + 2 * k, ranks)
        copies.append(remote(whole(r), whole(r), send_z.at[k], recv_z.at[k], (peer, c)))
        copies[-1].start()
    copies.append(remote(whole(r), whole(r), send_s.at[0], recv_s.at[0], (sibling, c)))
    copies[-1].start()
    half, columns = query_slice(c)
    fetches[2].wait()
    fetches[3].wait()
    own_query.wait()
    g_out[query_rows(c), :] = g_ref[half, columns]

    for h in range(KV_HEADS):
        cut = slice(h * LANES, (h + 1) * LANES)
        product = jnp.transpose(g_ref[:, cut].astype(f32) * o_ref[:, cut].astype(f32))
        sums = jnp.sum(product.reshape(MEMBERS, HEAD, rows), axis=1) * 0.125
        for u in range(rows // STRETCH):
            line = jnp.concatenate(
                [sums[m : m + 1, u * STRETCH : (u + 1) * STRETCH] for m in range(MEMBERS)], axis=1
            )
            each = part // STRETCH
            terms[h * halves + u // each, u % each : u % each + 1, :] = line
    for k in range(1, cols):
        peer = lax.rem(c + k, cols)
        copies.append(to_peer(k, 3, terms.at[peer], d_out.at[c], peer))
        copies[-1].start()
    d_out[c] = terms[c]

    for k in range(1, ranks // 2):
        source = lax.rem(r + ranks - 2 * k, ranks)
        peer = lax.rem(r + 2 * k, ranks)
        here = whole(source)
        remote(here, here, send_z.at[k], recv_z.at[k], (peer, c)).wait_recv()
        copies.append(remote(here, here, send_s.at[k], recv_s.at[k], (sibling, c)))
        copies[-1].start()
    for k in range(ranks // 2):
        here = whole(lax.rem(sibling + ranks - 2 * k, ranks))
        remote(here, here, send_s.at[k], recv_s.at[k], (sibling, c)).wait_recv()
    for k in range(1, cols):
        source = lax.rem(c + cols - k, cols)
        from_peer(k, 1, q_out.at[query_rows(source)]).wait_recv()
        from_peer(k, 2, g_out.at[query_rows(source)]).wait_recv()
        from_peer(k, 3, d_out.at[source]).wait_recv()
    for copy in copies:
        copy.wait_send()


def gather(queries, out_grad, outputs, keys, values, ranks, cols):
    rows = queries.shape[0]
    part = rows // (cols // KV_HEADS)
    bf16 = jnp.bfloat16
    vmem = pl.BlockSpec(memory_space=pltpu.VMEM)
    dma = pltpu.SemaphoreType.DMA
    return pl.pallas_call(
        functools.partial(gather_kernel, ranks, cols),
        out_shape=(
            jax.ShapeDtypeStruct((cols * part, LANES), bf16),
            jax.ShapeDtypeStruct((cols * part, LANES), bf16),
            jax.ShapeDtypeStruct((cols, 8, LANES), jnp.float32),
            jax.ShapeDtypeStruct((ranks * cols * rows, 2 * HEAD), bf16),
        ),
        in_specs=[pl.BlockSpec(memory_space=pltpu.HBM)] * 5,
        out_specs=(vmem,) * 4,
        scratch_shapes=[
            pltpu.VMEM((KV_HEADS, rows, 2 * HEAD), bf16),
            pltpu.VMEM((cols, 8, LANES), jnp.float32),
            pltpu.VMEM((rows, HEADS * HEAD), bf16),
            pltpu.VMEM((rows, HEADS * HEAD), bf16),
            pltpu.VMEM((rows, KV_HEADS * HEAD), bf16),
            pltpu.VMEM((rows, KV_HEADS * HEAD), bf16),
            dma((5,)),
            dma((cols, 4)), dma((cols, 4)),
            dma((ranks // 2,)), dma((ranks // 2,)),
            dma((ranks // 2,)), dma((ranks // 2,)),
        ],
        compiler_params=pltpu.CompilerParams(
            collective_id=0, has_side_effects=True, vmem_limit_bytes=GRANT
        ),
    )(queries, out_grad, outputs, keys, values)


def scatter_kernel(
    ranks, cols, dq_ref, dkv_ref, q_out, k_out, v_out,
    near, passing, far, share, last,
    send_q, recv_q, send_s, recv_s, send_z, recv_z, send_a, recv_a,
):
    f32, bf16 = jnp.float32, jnp.bfloat16
    r, c = lax.axis_index("qrow"), lax.axis_index("kcol")
    sibling = r + 1 - 2 * lax.rem(r, 2)
    rows = q_out.shape[0]
    halves = cols // KV_HEADS
    part = rows // halves
    block = cols * rows
    steps = ranks // 2
    greet(ranks, cols)

    def span(rank):
        return pl.ds(pl.multiple_of(rank * block, block), block)

    def query_rows(col):
        return pl.ds(pl.multiple_of(col * part, part), part)

    def query_slice(col):
        half = pl.ds(pl.multiple_of(lax.rem(col, halves) * part, part), part)
        return half, pl.ds(pl.multiple_of((col // halves) * LANES, LANES), LANES)

    copies = []
    order = list(range(1, steps)) + [0]
    for k in order:
        target = lax.rem(sibling + 2 * k, ranks)
        copies.append(
            remote(dkv_ref.at[span(target)], near.at[k], send_s.at[k], recv_s.at[k], (sibling, c))
        )
        copies[-1].start()
    for k in order:
        peer = lax.rem(r + 2 * k, ranks)
        remote(near.at[k], near.at[k], send_s.at[k], recv_s.at[k], (sibling, c)).wait_recv()
        both = dkv_ref[span(peer), :].astype(f32) + near[k].astype(f32)
        if k:
            passing[k] = both.astype(bf16)
            copies.append(
                remote(passing.at[k], far.at[k], send_z.at[k], recv_z.at[k], (peer, c))
            )
            copies[-1].start()
    half, columns = query_slice(c)
    for k in range(1, cols):
        peer = lax.rem(c + k, cols)
        copies.append(
            remote(
                dq_ref.at[query_rows(peer)], q_out.at[half, columns],
                send_q.at[k], recv_q.at[k], (r, peer),
            )
        )
        copies[-1].start()
    q_out[half, columns] = dq_ref[query_rows(c), :]
    total = both
    for k in range(1, steps):
        peer = lax.rem(r + 2 * k, ranks)
        remote(far.at[k], far.at[k], send_z.at[k], recv_z.at[k], (peer, c)).wait_recv()
        total = total + far[k].astype(f32)
    share[...] = total.astype(bf16)

    def share_rows(col):
        return pl.ds(pl.multiple_of(col * rows, rows), rows)

    for k in range(1, cols):
        peer = lax.rem(c + k, cols)
        copies.append(
            remote(share.at[share_rows(peer)], last.at[c], send_a.at[k], recv_a.at[k], (r, peer))
        )
        copies[-1].start()
    last[c] = share[share_rows(c), :]
    for k in range(1, cols):
        peer = lax.rem(c + k, cols)
        here = last.at[lax.rem(c + cols - k, cols)]
        remote(here, here, send_a.at[k], recv_a.at[k], (r, peer)).wait_recv()
    k_parts, v_parts = [], []
    for h in range(KV_HEADS):
        whole = last[h * halves].astype(f32)
        for other in range(1, halves):
            whole = whole + last[h * halves + other].astype(f32)
        v_parts.append(whole[:, :HEAD])
        k_parts.append(whole[:, HEAD:])
    k_out[...] = jnp.concatenate(k_parts, axis=1).astype(bf16)
    v_out[...] = jnp.concatenate(v_parts, axis=1).astype(bf16)
    for k in range(1, cols):
        peer = lax.rem(c + k, cols)
        half, columns = query_slice(lax.rem(c + cols - k, cols))
        here = q_out.at[half, columns]
        remote(dq_ref.at[query_rows(peer)], here, send_q.at[k], recv_q.at[k], (r, peer)).wait_recv()
    for copy in copies:
        copy.wait_send()


def scatter(dq, dkv, rows, ranks, cols):
    bf16 = jnp.bfloat16
    vmem = pl.BlockSpec(memory_space=pltpu.VMEM)
    dma = pltpu.SemaphoreType.DMA
    block = cols * rows
    return pl.pallas_call(
        functools.partial(scatter_kernel, ranks, cols),
        out_shape=(
            jax.ShapeDtypeStruct((rows, HEADS * HEAD), bf16),
            jax.ShapeDtypeStruct((rows, KV_HEADS * HEAD), bf16),
            jax.ShapeDtypeStruct((rows, KV_HEADS * HEAD), bf16),
        ),
        in_specs=[vmem] * 2,
        out_specs=(vmem,) * 3,
        scratch_shapes=[
            pltpu.VMEM((ranks // 2, block, 2 * HEAD), bf16),
            pltpu.VMEM((ranks // 2, block, 2 * HEAD), bf16),
            pltpu.VMEM((ranks // 2, block, 2 * HEAD), bf16),
            pltpu.VMEM((block, 2 * HEAD), bf16),
            pltpu.VMEM((cols, rows, 2 * HEAD), bf16),
            dma((cols,)), dma((cols,)),
            dma((ranks // 2,)), dma((ranks // 2,)),
            dma((ranks // 2,)), dma((ranks // 2,)),
            dma((cols,)), dma((cols,)),
        ],
        compiler_params=pltpu.CompilerParams(
            collective_id=1, has_side_effects=True, vmem_limit_bytes=40 * 1024 * 1024
        ),
    )(dq, dkv)


def per_device(queries, keys, values, outputs, out_grad, positions):
    rows = queries.shape[0]
    ranks = lax.axis_size("qrow")
    cols = lax.axis_size("kcol")
    q, g, d, kv = gather(queries, out_grad, outputs, keys, values, ranks, cols)
    dq, dkv = attention(positions, q, g, d, kv, ranks, cols)
    return scatter(dq, dkv, rows, ranks, cols)


def solution(mesh):
    in_specs = (
        P(("kcol", "qrow"), None),
        P(("qrow", "kcol"), None),
        P(("qrow", "kcol"), None),
        P(("kcol", "qrow"), None),
        P(("kcol", "qrow"), None),
        P(),
    )
    out_specs = (P(("kcol", "qrow"), None), P(("qrow", "kcol"), None), P(("qrow", "kcol"), None))
    return jax.shard_map(
        per_device, mesh=mesh, in_specs=in_specs, out_specs=out_specs, check_vma=False
    )
```
